32 devices in a mesh: grp: 2 (over y), cand: 8 (over z, x), head: 2 (over core).
Axes of the slice: x: 2, y: 2, z: 4, core: 2. Of those that a mesh axis runs over, the one named last changes fastest.
Arguments:
- queries: bfloat16 [8192, 2560], P(('grp', 'cand'), 'head'), parts along dimension 0, may hold values from -130 to 130
- keys: bfloat16 [8192, 512], P(('grp', 'cand'), 'head'), parts along dimension 0, may hold values from -5 to 5
- values: bfloat16 [8192, 512], P(('grp', 'cand'), 'head'), parts along dimension 0, may hold values from -6 to 6
- lengths: int32 [16], P('grp'), parts along dimension 0, may hold values from 257 to 512, as said below
- winners: int32 [8], P('grp'), parts along dimension 0, may hold values from 0 to 1
- score_weight: float32 [2560], P('head'), may hold values from -16 to 16
Outputs:
- first_round: bfloat16 [8192, 2560], P(('grp', 'cand'), 'head'), parts along dimension 0
- second_round: bfloat16 [4096, 2560], P(('grp', 'cand'), 'head'), parts along dimension 0
- first_score: float32 [16], P(('grp', 'cand')), parts along dimension 0
- final_round_score: float32 [16], P(('grp', 'cand')), parts along dimension 0
The draws below stay inside these ranges and needn't reach their ends.
There are 2 independent parts, one for each index of `grp`. The reference program is written for one: setup_inputs(seed, part) draws one part's arguments, and reference() takes and returns one part's arrays. A program takes and returns all parts, laid end to end along the dimension named above; an argument that names none is the same for every part. Nothing has to cross between parts.
Inputs may be any that keep to these rules, and one draw needn't show every extreme that they name: lengths of all candidates lie in this range; some candidate uses all 512 slots. `winners`: 0 picks the even member 2 j of pair j, 1 the odd one.
All inputs are finite; a program needn't handle non-finite values.
Results may differ from the reference program's by a relative error of at most 0.0049.
Values may be sent and summed in bfloat16 or wider, within the bound.
No kernel may reach another device: no remote copies, remote signals or barrier semaphores. Data moves between devices by JAX's collectives and lax.ppermute only.
A program may use at most 128 MiB of HBM per device.

```python
import jax
import jax.numpy as jnp
from jax import lax

HQ = 20
KVH = 4
HD = 128
SPAN = 512
CANDS = 8


def shared_keys(key):
    drawn = jax.random.truncated_normal(jax.random.fold_in(key, 11), -5.0, 5.0, (CANDS, SPAN, KVH, HD), jnp.float32)
    return drawn


def draw_keys(key, part):
    return shared_keys(key).reshape(CANDS * SPAN, KVH * HD).astype(jnp.bfloat16)


def draw_queries(key, part):
    base = 1.5 * jax.random.truncated_normal(jax.random.fold_in(key, 12), -5.0, 5.0, (CANDS, SPAN, HQ, HD), jnp.float32)
    return base.reshape(CANDS * SPAN, HQ * HD).astype(jnp.bfloat16)


def draw_lengths(key, part):
    drawn = jax.random.randint(jax.random.fold_in(key, 13), (CANDS,), SPAN // 2 + 1, SPAN + 1, dtype=jnp.int32)
    fullest = jax.random.randint(jax.random.fold_in(key, 14), (), 0, CANDS, dtype=jnp.int32)
    return drawn.at[fullest].set(SPAN)


def draw_score_weight(key, part):
    count = HQ * HD
    ramp = 1.0 + 2.0 * jnp.arange(count, dtype=jnp.float32) / (count - 1)
    drawn = jax.random.truncated_normal(jax.random.fold_in(key, 15), -5.0, 5.0, (count,), jnp.float32) * ramp
    return drawn


def touch_ends(values, stream_key, smallest, high):
    longest = values.shape.index(max(values.shape))
    spots = []
    for shift in (0, 1):
        where = [jax.random.randint(jax.random.fold_in(stream_key, axis), (), 0, length) for axis, length in enumerate(values.shape)]
        where[longest] = (where[longest] + shift) % values.shape[longest]
        spots.append(tuple(where))
    return values.at[spots[0]].set(smallest).at[spots[1]].set(high)


def block_scale(own_key, shape, pieces, low, top_value):
    def one(position, blocks):
        heights = jax.random.uniform(jax.random.fold_in(jax.random.fold_in(own_key, 6), position), (blocks,), jnp.float32, low / len(pieces), top_value / len(pieces))
        return jnp.repeat(jnp.exp(heights), shape[position] // blocks).reshape((-1,) + (1,) * (len(shape) - position - 1))

    factor_of = one(*pieces[0])
    for cut in pieces[1:]:
        factor_of = factor_of * one(*cut)
    return factor_of


def gaussian(own_key, extent, scale, bound, cuts=(), held_as=jnp.bfloat16):
    loudness = block_scale(own_key, extent, cuts, -0.22, 0.18) if cuts else 1.0
    array = jax.random.normal(own_key, extent, jnp.float32) * scale * loudness
    return jnp.minimum(jnp.maximum(array, -bound), bound).astype(held_as)


def setup_inputs(seed: int = 0, part: int = 0) -> dict:
    seeds = jax.random.split(jax.random.key(seed), 7)
    part_splits = jax.random.split(jax.random.fold_in(seeds[6], part), 7)
    return {
        "queries": draw_queries(jax.random.fold_in(jax.random.fold_in(seeds[6], part), 71), part),
        "keys": draw_keys(jax.random.fold_in(jax.random.fold_in(seeds[6], part), 71), part),
        "values": gaussian(part_splits[2], (CANDS * SPAN, KVH * HD), 1.0, 6.0, ((0, 8), (1, 2))),
        "lengths": draw_lengths(jax.random.fold_in(jax.random.fold_in(seeds[6], part), 71), part),
        "winners": touch_ends(jax.random.randint(part_splits[4], (CANDS // 2,), 0, 2), jax.random.fold_in(part_splits[4], 1), 0, 1).astype(jnp.int32),
        "score_weight": draw_score_weight(jax.random.fold_in(seeds[6], 71), part),
    }


def attend_spans(query_rows, key_rows, value_rows, key_valid, valid_row_mask):
    row_count = query_rows.shape[0]
    ratio = HQ // KVH
    grouped_q = query_rows.reshape(row_count, KVH, ratio, HD).transpose(1, 0, 2, 3)
    grouped_k = key_rows.reshape(-1, KVH, HD).transpose(1, 0, 2)
    grouped_v = value_rows.reshape(-1, KVH, HD).transpose(1, 0, 2)

    def one_group(operands):
        queries_g, keys_g, values_g = operands
        scores = jnp.einsum("qrd,kd->rqk", queries_g.astype(jnp.float32), keys_g.astype(jnp.float32)) * (HD ** -0.5)
        scores = jnp.where(key_valid[None, None, :], scores, -jnp.inf)
        peak = jnp.max(scores, axis=2, keepdims=True)
        exps = jnp.exp(scores - peak)
        weights = (exps / jnp.sum(exps, axis=2, keepdims=True)).astype(jnp.bfloat16)
        return jnp.einsum("rqk,kd->qrd", weights.astype(jnp.float32), values_g.astype(jnp.float32))

    outputs = lax.map(one_group, (grouped_q, grouped_k, grouped_v))
    merged = outputs.transpose(1, 0, 2, 3).reshape(row_count, HQ * HD)
    return (merged * valid_row_mask[:, None].astype(jnp.float32)).astype(jnp.bfloat16)


def reference(queries, keys, values, lengths, winners, score_weight):
    cand_q = queries.reshape(CANDS, SPAN, HQ * HD)
    cand_k = keys.reshape(CANDS, SPAN, KVH * HD)
    cand_v = values.reshape(CANDS, SPAN, KVH * HD)
    span_positions = jnp.arange(SPAN, dtype=jnp.int32)
    valid = span_positions[None, :] < lengths[:, None]

    def match_result(pairing_identifiers):
        own = pairing_identifiers[0]
        rival = pairing_identifiers[1]
        key_rows = jnp.concatenate([cand_k[own], cand_k[rival]], axis=0)
        value_rows = jnp.concatenate([cand_v[own], cand_v[rival]], axis=0)
        key_valid = jnp.concatenate([valid[own], valid[rival]], axis=0)
        return attend_spans(cand_q[own], key_rows, value_rows, key_valid, valid[own])

    everyone = jnp.arange(CANDS, dtype=jnp.int32)
    first = lax.map(match_result, jnp.stack([everyone, jnp.bitwise_xor(everyone, 1)], axis=1))
    pairing_identifiers = jnp.arange(CANDS // 2, dtype=jnp.int32)
    remaining_candidates = 2 * pairing_identifiers + winners
    challengers = remaining_candidates[jnp.bitwise_xor(pairing_identifiers, 1)]
    later_round = lax.map(match_result, jnp.stack([remaining_candidates, challengers], axis=1))
    weight = score_weight.astype(jnp.float32)
    first_totals = jnp.sum(first.astype(jnp.float32) * weight, axis=(1, 2))
    first_score = first_totals / lengths.astype(jnp.float32)
    final_round_totals = jnp.sum(later_round.astype(jnp.float32) * weight, axis=(1, 2))
    final_round_score = jnp.repeat(final_round_totals / lengths[remaining_candidates].astype(jnp.float32), 2)
    return (first.reshape(CANDS * SPAN, HQ * HD), later_round.reshape(CANDS // 2 * SPAN, HQ * HD), first_score, final_round_score)
```

```python
import functools

import jax
import jax.numpy as jnp
from jax import lax
from jax.experimental import pallas as pl
from jax.experimental.pallas import tpu as pltpu
from jax.sharding import PartitionSpec as P

HD = 128
LANES = 128
FACTOR = HD ** (-0.5) * 1.4426950408889634
BARRED = -1e30
VMEM_LIMIT = 40 * 1024 * 1024
ANY = pl.BlockSpec(memory_space=pl.ANY)
SMEM = pl.BlockSpec(memory_space=pltpu.SMEM)


def from_partner(value, axis, stride):
    return lax.ppermute(value, axis, [(i, i ^ 1 << stride) for i in range(lax.axis_size(axis))])


def fill_constant_columns(k_buf, v_buf, valid_a, valid_b):
    span = k_buf.shape[0] // 2
    row = lax.broadcasted_iota(jnp.int32, (span, LANES), 0)
    first_lane = lax.broadcasted_iota(jnp.int32, (span, LANES), 1) == 0
    for place, valid in ((0, valid_a), (1, valid_b)):
        bar = jnp.where(first_lane & (row >= valid), BARRED, 0.0)
        k_buf[place * span : (place + 1) * span, HD:] = bar.astype(k_buf.dtype)
    v_buf[:, HD:] = jnp.ones((2 * span, LANES), v_buf.dtype)


def attend_rows(q, k_buf, v_buf, valid_rows, first_row):
    rows = q.shape[0]
    lane = lax.broadcasted_iota(jnp.int32, (rows, LANES), 1)
    one_lane = jnp.where(lane == 0, 1.0, 0.0).astype(q.dtype)
    wide_q = jnp.concatenate([q, one_lane], axis=1)
    scores = lax.dot_general(
        wide_q, k_buf[...], (((1,), (1,)), ((), ())), preferred_element_type=jnp.float32
    )
    peak = jnp.max(scores, axis=1, keepdims=True)
    exps = jnp.exp2((scores - peak) * FACTOR).astype(v_buf.dtype)
    both = jnp.dot(exps, v_buf[...], preferred_element_type=jnp.float32)
    output = both[:, :HD] / both[:, HD:]
    row = lax.broadcasted_iota(jnp.int32, (rows, LANES), 0) + first_row
    return jnp.where(row < valid_rows, output, 0.0).astype(q.dtype)


def attend_kernel(
    group, ratio, row_block, picked,
    info_ref, weight_ref, q_ref, other_q_ref, ka_ref, va_ref, kb_ref, vb_ref, prior_ref,
    out_ref, part_ref,
    q_buf, k_buf, v_buf, out_buf, q_sems, k_sems, out_sems,
):
    rows = q_buf.shape[0]
    span = k_buf.shape[0] // 2
    first_row = pl.multiple_of(info_ref[2], 16)
    columns = [pl.ds((group * ratio + h) * HD, HD) for h in range(ratio)]
    near = [pl.ds(h * HD, HD) for h in range(ratio)]
    kv_columns = pl.ds(group * HD, HD)

    def kv_copy(index):
        ref, buf, place = ((ka_ref, k_buf, 0), (kb_ref, k_buf, 1), (va_ref, v_buf, 0), (vb_ref, v_buf, 1))[index]
        source = ref if ref.shape[1] == HD else ref.at[:, kv_columns]
        return pltpu.make_async_copy(source, buf.at[pl.ds(place * span, span), pl.ds(0, HD)], k_sems.at[index])

    def own_q(h):
        return pltpu.make_async_copy(
            q_ref.at[pl.ds(first_row, rows), columns[h]], q_buf.at[:, near[h]], q_sems.at[h]
        )

    def other_q(h):
        return pltpu.make_async_copy(other_q_ref.at[:, near[h]], q_buf.at[:, near[h]], q_sems.at[h])

    kv_copy(0).start()
    kv_copy(1).start()
    if picked:
        @pl.when(info_ref[3] == 1)
        def _():
            for h in range(ratio):
                own_q(h).start()

        @pl.when(info_ref[3] != 1)
        def _():
            for h in range(ratio):
                other_q(h).start()
    else:
        for h in range(ratio):
            own_q(h).start()
    kv_copy(2).start()
    kv_copy(3).start()
    fill_constant_columns(k_buf, v_buf, info_ref[0], info_ref[1])
    for index in range(4):
        kv_copy(index).wait()

    total = jnp.zeros((8, LANES), jnp.float32)
    for h in range(ratio):
        own_q(h).wait()
        weight = weight_ref[:, (group * ratio + h) * HD : (group * ratio + h + 1) * HD]
        head_total = jnp.zeros((8, LANES), jnp.float32)
        for start in range(0, rows, row_block):
            output = attend_rows(
                q_buf[start : start + row_block, h * HD : (h + 1) * HD], k_buf, v_buf, info_ref[0], first_row + start
            )
            out_buf[start : start + row_block, h * HD : (h + 1) * HD] = output
            head_total += jnp.sum(output.astype(jnp.float32).reshape(row_block // 8, 8, LANES), axis=0)
        total += head_total * weight
        pltpu.make_async_copy(out_buf.at[:, near[h]], out_ref.at[:, columns[h]], out_sems.at[h]).start()
    part_ref[...] = jnp.full(part_ref.shape, jnp.sum(total), jnp.float32)
    for h in range(ratio):
        pltpu.make_async_copy(out_buf.at[:, near[h]], out_ref.at[:, columns[h]], out_sems.at[h]).wait()


def attend(group, rows, info, weight, q, other_q, ka, va, kb, vb, prior):
    span = ka.shape[0]
    groups = ka.shape[1] // HD
    ratio = q.shape[1] // HD // groups
    row_block = min(rows, 256)
    picked = other_q is not None
    out_shape = (jax.ShapeDtypeStruct((rows, q.shape[1]), q.dtype), jax.ShapeDtypeStruct((8, LANES), jnp.float32))
    if not picked:
        other_q = q
    aliased = prior is not None
    if not aliased:
        prior = jnp.zeros((8, LANES), jnp.float32)
    flops = 4 * rows * ratio * HD * 2 * span
    return pl.pallas_call(
        functools.partial(attend_kernel, group, ratio, row_block, picked),
        out_shape=out_shape,
        in_specs=[SMEM, pl.BlockSpec(memory_space=pltpu.VMEM)] + [ANY] * 7,
        out_specs=(ANY, pl.BlockSpec(memory_space=pltpu.VMEM)),
        input_output_aliases={8: 0} if aliased else {},
        scratch_shapes=[
            pltpu.VMEM((rows, ratio * HD), q.dtype),
            pltpu.VMEM((2 * span, HD + LANES), ka.dtype),
            pltpu.VMEM((2 * span, HD + LANES), va.dtype),
            pltpu.VMEM((rows, ratio * HD), q.dtype),
            pltpu.SemaphoreType.DMA((ratio,)),
            pltpu.SemaphoreType.DMA((4,)),
            pltpu.SemaphoreType.DMA((ratio,)),
        ],
        compiler_params=pltpu.CompilerParams(vmem_limit_bytes=VMEM_LIMIT),
        cost_estimate=pl.CostEstimate(
            flops=flops, bytes_accessed=4 * rows * ratio * HD, transcendentals=rows * ratio * 2 * span
        ),
    )(info, weight, q, other_q, ka, va, kb, vb, prior)


def body(queries, keys, values, lengths, winners, score_weight):
    span = queries.shape[0]
    half = span // 2
    groups = keys.shape[1] // HD
    width = queries.shape[1] // groups
    device = lax.axis_index("cand")
    bit = device % 2
    pair = device // 2
    partner = jnp.bitwise_xor(device, 1)
    winner = winners[pair]
    survivor = 2 * pair + winner
    rival_pair = jnp.bitwise_xor(pair, 1)
    rival = 2 * rival_pair + winners[rival_pair]
    won = bit == winner
    weight = score_weight.reshape(1, -1)
    first_info = jnp.stack([lengths[device], lengths[partner], jnp.int32(0), jnp.int32(1)])
    second_info = jnp.stack([lengths[survivor], lengths[rival], bit * half, won.astype(jnp.int32)])

    def group_part(array, g, size):
        return array[:, g * size : (g + 1) * size]

    companion_keys = from_partner(keys, "cand", 0)
    companion_values = [from_partner(group_part(values, g, HD), "cand", 0) for g in range(groups)]
    sent_rows = lax.dynamic_slice_in_dim(queries, (1 - bit) * half, half, 0)
    partner_queries = [from_partner(group_part(sent_rows, g, width), "cand", 0) for g in range(groups)]

    survivor_keys = jnp.where(won, keys, companion_keys)
    rival_keys = from_partner(survivor_keys, "cand", 1)
    survivor_values, rival_values = [], []
    for g in range(groups):
        survivor_values.append(jnp.where(won, group_part(values, g, HD), companion_values[g]))
        rival_values.append(from_partner(survivor_values[g], "cand", 1))

    first, first_part = None, 0.0
    for g in range(groups):
        first, part = attend(
            g, span, first_info, weight, queries, None, keys, values, companion_keys, companion_values[g], first
        )
        first_part += part[0, 0]
    second, second_part = None, 0.0
    for g in range(groups):
        second, part = attend(
            g, half, second_info, weight, queries, partner_queries[g],
            survivor_keys, survivor_values[g], rival_keys, rival_values[g], second,
        )
        second_part += part[0, 0]

    first_total, second_total = lax.psum((first_part.reshape(1), second_part.reshape(1)), "head")
    other_half = from_partner(second_total, "cand", 0)
    first_score = first_total / lengths[device].astype(jnp.float32)
    final_round_score = (second_total + other_half) / lengths[survivor].astype(jnp.float32)
    return first, second, first_score, final_round_score


def solution(mesh):
    in_specs = (
        P(("grp", "cand"), "head"),
        P(("grp", "cand"), "head"),
        P(("grp", "cand"), "head"),
        P("grp"),
        P("grp"),
        P("head"),
    )
    out_specs = (
        P(("grp", "cand"), "head"),
        P(("grp", "cand"), "head"),
        P(("grp", "cand")),
        P(("grp", "cand")),
    )
    return jax.shard_map(body, mesh=mesh, in_specs=in_specs, out_specs=out_specs, check_vma=False)
```

```python
import functools

import jax
import jax.numpy as jnp
from jax import lax
from jax.experimental import pallas as pl
from jax.experimental.pallas import tpu as pltpu
from jax.sharding import PartitionSpec as P

HD = 128
LANES = 128
LOG2E = 1.4426950408889634
FACTOR = HD ** (-0.5) * LOG2E
BARRED = -1e30
VMEM_LIMIT = 12 * 1024 * 1024
ANY = pl.BlockSpec(memory_space=pl.ANY)
VMEM = pl.BlockSpec(memory_space=pltpu.VMEM)
SMEM = pl.BlockSpec(memory_space=pltpu.SMEM)


def from_partner(value, axis, stride):
    return lax.ppermute(value, axis, [(i, i ^ 1 << stride) for i in range(lax.axis_size(axis))])


class Place:
    def __init__(self, lengths_ref, winners_ref):
        device = lax.axis_index("cand")
        self.bit = device & 1
        pair = device >> 1
        self.winner = winners_ref[pair]
        self.won = self.bit == self.winner
        rival_pair = pair ^ 1
        self.own_valid = lengths_ref[device]
        self.partner_valid = lengths_ref[device ^ 1]
        self.survivor_valid = lengths_ref[2 * pair + self.winner]
        self.rival_valid = lengths_ref[2 * rival_pair + winners_ref[rival_pair]]


def load_span(k_buf, v_buf, k_ref, v_ref, group, valid, start):
    span = k_ref.shape[0]
    k_columns = slice(group * HD, (group + 1) * HD)
    v_columns = k_columns if v_ref.shape[1] == k_ref.shape[1] else slice(0, HD)
    rows = slice(start, start + span)
    row = lax.broadcasted_iota(jnp.int32, (span, LANES), 0)
    first_lane = lax.broadcasted_iota(jnp.int32, (span, LANES), 1) == 0
    k_buf[rows, :HD] = k_ref[:, k_columns]
    k_buf[rows, HD:] = jnp.where(first_lane & (row >= valid), BARRED, 0.0).astype(k_buf.dtype)
    v_buf[rows, :HD] = v_ref[:, v_columns]
    v_buf[rows, HD:] = jnp.ones((span, LANES), v_buf.dtype)


def score_rows(q, k_buf):
    lane = lax.broadcasted_iota(jnp.int32, (q.shape[0], LANES), 1)
    one_lane = jnp.where(lane == 0, 1.0, 0.0).astype(q.dtype)
    wide_q = jnp.concatenate([q, one_lane], axis=1)
    return lax.dot_general(wide_q, k_buf[...], (((1,), (1,)), ((), ())), preferred_element_type=jnp.float32)


def weigh(scores, peak, v_buf):
    wide_peak = jnp.concatenate([peak] * (scores.shape[1] // LANES), axis=1)
    exps = jnp.exp2(scores * FACTOR - wide_peak).astype(v_buf.dtype)
    both = jnp.dot(exps, v_buf[...], preferred_element_type=jnp.float32)
    return both[:, :HD], both[:, HD:]


def peak_of(scores):
    peak = jnp.max(scores, axis=1, keepdims=True) * FACTOR
    return jnp.broadcast_to(peak, (scores.shape[0], LANES))


def finish(above, below, valid_rows, first_row, dtype):
    row = lax.broadcasted_iota(jnp.int32, above.shape, 0) + first_row
    return jnp.where(row < valid_rows, above / below, 0.0).astype(dtype)


def own_kernel(ratio, block, cuts, lengths_ref, q_ref, k_ref, v_ref, o_ref, mass_ref, *rest):
    piece_refs, (k_buf, v_buf) = rest[: len(cuts)], rest[len(cuts) :]
    device = lax.axis_index("cand")
    half = q_ref.shape[0] // 2
    sent = pl.ds(pl.multiple_of((1 - (device & 1)) * half, half), half)
    for piece_ref, (_, low, high) in zip(piece_refs, cuts):
        piece_ref[...] = q_ref[sent, low * HD : high * HD]
    for group in range(k_ref.shape[1] // HD):
        load_span(k_buf, v_buf, k_ref, v_ref, group, lengths_ref[device], 0)
        for head in range(group * ratio, (group + 1) * ratio):
            columns = slice(head * HD, (head + 1) * HD)
            for start in range(0, q_ref.shape[0], block):
                rows = slice(start, start + block)
                scores = score_rows(q_ref[rows, columns], k_buf)
                peak = peak_of(scores)
                above, below = weigh(scores, peak, v_buf)
                o_ref[rows, columns] = above / below
                mass_ref[rows, columns] = peak + jnp.log(below) * LOG2E


def choose_kernel(lengths_ref, winners_ref, own_ref, companion_ref, *out_refs):
    place = Place(lengths_ref, winners_ref)
    for won, ref in ((True, own_ref), (False, companion_ref)):
        @pl.when(place.won == won)
        def _():
            start = 0
            for out_ref in out_refs:
                out_ref[...] = ref[:, start : start + out_ref.shape[1]]
                start += out_ref.shape[1]


def join_head(columns, block, valid_rows, q_ref, o_ref, mass_ref, weight_ref, k_buf, v_buf, out_buf, out_columns):
    total = jnp.zeros((8, LANES), jnp.float32)
    for start in range(0, q_ref.shape[0], block):
        rows = slice(start, start + block)
        scores = score_rows(q_ref[rows, columns], k_buf)
        mass = mass_ref[rows, columns]
        peak = jnp.maximum(mass, peak_of(scores))
        above, below = weigh(scores, peak, v_buf)
        keep = jnp.exp2(mass - peak)
        output = finish(above + o_ref[rows, columns] * keep, below + keep, valid_rows, start, out_buf.dtype)
        out_buf[rows, out_columns] = output
        total += jnp.sum(output.astype(jnp.float32).reshape(block // 8, 8, LANES), axis=0)
    return total * weight_ref[:, columns]


def first_kernel(
    ratio, block, lengths_ref, weight_ref, q_ref, o_ref, mass_ref, k_ref, v_ref,
    out_ref, part_ref, k_buf, v_buf, out_buf, out_sems,
):
    device = lax.axis_index("cand")
    heads = q_ref.shape[1] // HD

    def out_copy(head):
        columns = pl.ds(head * HD, HD)
        return pltpu.make_async_copy(out_buf.at[:, columns], out_ref.at[:, columns], out_sems.at[head])

    total = jnp.zeros((8, LANES), jnp.float32)
    for group in range(heads // ratio):
        load_span(k_buf, v_buf, k_ref, v_ref, group, lengths_ref[device ^ 1], 0)
        for head in range(group * ratio, (group + 1) * ratio):
            columns = slice(head * HD, (head + 1) * HD)
            total += join_head(
                columns, block, lengths_ref[device], q_ref, o_ref, mass_ref, weight_ref, k_buf, v_buf, out_buf, columns
            )
            out_copy(head).start()
    part_ref[...] = jnp.full(part_ref.shape, jnp.sum(total), jnp.float32)
    for head in range(heads):
        out_copy(head).wait()


def winner_kernel(
    group, ratio, block, lengths_ref, winners_ref, weight_ref, q_ref, o_ref, mass_ref, k_ref, v_ref, before_ref, prior_ref,
    out_ref, part_ref, k_buf, v_buf, out_buf, out_sems,
):
    place = Place(lengths_ref, winners_ref)
    half = out_buf.shape[0] // 2
    kept = pl.ds(pl.multiple_of(place.bit * half, half), half)

    def out_copy(h):
        return pltpu.make_async_copy(
            out_buf.at[kept, pl.ds(h * HD, HD)], out_ref.at[:, pl.ds((group * ratio + h) * HD, HD)], out_sems.at[h]
        )

    @pl.when(place.won)
    def _():
        load_span(k_buf, v_buf, k_ref, v_ref, group, place.rival_valid, 0)
        total = jnp.zeros((8, LANES), jnp.float32)
        for h in range(ratio):
            columns = slice((group * ratio + h) * HD, (group * ratio + h + 1) * HD)
            total += join_head(
                columns, block, place.own_valid, q_ref, o_ref, mass_ref, weight_ref, k_buf, v_buf,
                out_buf, slice(h * HD, (h + 1) * HD),
            )
            out_copy(h).start()
        part = jnp.full(part_ref.shape, jnp.sum(total), jnp.float32)
        part_ref[...] = part + before_ref[...] if group else part
        for h in range(ratio):
            out_copy(h).wait()

    @pl.when(jnp.logical_not(place.won))
    def _():
        part_ref[...] = jnp.zeros(part_ref.shape, jnp.float32)


def loser_kernel(
    group, first_head, lengths_ref, winners_ref, q_ref, ka_ref, va_ref, kb_ref, vb_ref, prior_ref,
    out_ref, k_buf, v_buf, out_buf, out_sems,
):
    place = Place(lengths_ref, winners_ref)
    rows, span = q_ref.shape[0], ka_ref.shape[0]
    heads = q_ref.shape[1] // HD

    def out_copy(h):
        return pltpu.make_async_copy(
            out_buf.at[:, pl.ds(h * HD, HD)], out_ref.at[:, pl.ds((first_head + h) * HD, HD)], out_sems.at[h]
        )

    @pl.when(jnp.logical_not(place.won))
    def _():
        load_span(k_buf, v_buf, ka_ref, va_ref, group, place.partner_valid, 0)
        load_span(k_buf, v_buf, kb_ref, vb_ref, group, place.rival_valid, span)
        for h in range(heads):
            columns = slice(h * HD, (h + 1) * HD)
            scores = score_rows(q_ref[:, columns], k_buf)
            above, below = weigh(scores, peak_of(scores), v_buf)
            out_buf[:, columns] = finish(above, below, place.partner_valid, place.bit * rows, out_buf.dtype)
            out_copy(h).start()
        for h in range(heads):
            out_copy(h).wait()


def total_kernel(
    lengths_ref, winners_ref, first_ref, first_beside_ref, part_ref, beside_ref, across_ref, across_beside_ref,
    first_score_ref, final_score_ref,
):
    place = Place(lengths_ref, winners_ref)
    first = (first_ref[...] + first_beside_ref[...]) / place.own_valid.astype(jnp.float32)
    own = part_ref[...] + beside_ref[...]
    partner = across_ref[...] + across_beside_ref[...]
    final = jnp.where(place.won, own, partner) / place.survivor_valid.astype(jnp.float32)
    first_score_ref[0] = jnp.max(first)
    final_score_ref[0] = jnp.max(final)


def kernel_call(kernel, operands, in_specs, out_shape, out_specs, scratch=(), flops=0, aliases=None):
    return pl.pallas_call(
        kernel,
        out_shape=out_shape,
        in_specs=in_specs,
        out_specs=out_specs,
        scratch_shapes=scratch,
        input_output_aliases=aliases or {},
        compiler_params=pltpu.CompilerParams(vmem_limit_bytes=VMEM_LIMIT),
        cost_estimate=pl.CostEstimate(flops=flops, bytes_accessed=flops // 256, transcendentals=flops // 512),
    )(*operands)


def body(queries, keys, values, lengths, winners, score_weight):
    span, width = queries.shape
    half = span // 2
    heads = width // HD
    groups = keys.shape[1] // HD
    ratio = heads // groups
    block = min(span, 256)
    dtype = queries.dtype
    weight = score_weight.reshape(1, -1)
    share = 4 * span * span * HD
    part_shape = jax.ShapeDtypeStruct((8, LANES), jnp.float32)
    second_shape = jax.ShapeDtypeStruct((half, width), dtype)

    def buffers(spans):
        return [pltpu.VMEM((spans * span, HD + LANES), dtype)] * 2

    companion_keys = from_partner(keys, "cand", 0)
    companion_values = from_partner(values, "cand", 0)

    cuts = []
    for g in range(groups):
        middle = ratio if g < groups - 1 else (ratio + 1) // 2
        cuts.append((g, g * ratio, g * ratio + middle))
        if middle < ratio:
            cuts.append((g, g * ratio + middle, (g + 1) * ratio))
    piece_shapes = tuple(jax.ShapeDtypeStruct((half, (high - low) * HD), dtype) for _, low, high in cuts)
    partial = jax.ShapeDtypeStruct((span, width), jnp.float32)
    own_output, own_mass, *sent = kernel_call(
        functools.partial(own_kernel, ratio, block, cuts),
        (lengths, queries, keys, values),
        [SMEM, VMEM, VMEM, VMEM],
        (partial, partial) + piece_shapes,
        (VMEM,) * (2 + len(cuts)),
        buffers(1),
        share * heads,
    )
    pieces = [from_partner(piece, "cand", 0) for piece in sent]

    def choose(own, companion, parts):
        shape = jax.ShapeDtypeStruct((span, own.shape[1] // parts), dtype)
        return kernel_call(
            choose_kernel, (lengths, winners, own, companion), [SMEM, SMEM, VMEM, VMEM], (shape,) * parts, (VMEM,) * parts
        )

    rival_keys = from_partner(choose(keys, companion_keys, 1)[0], "cand", 1)
    rival_values = [from_partner(part, "cand", 1) for part in choose(values, companion_values, groups)]

    first, first_part = kernel_call(
        functools.partial(first_kernel, ratio, block),
        (lengths, weight, queries, own_output, own_mass, companion_keys, companion_values),
        [SMEM] + [VMEM] * 6,
        (jax.ShapeDtypeStruct((span, width), dtype), part_shape),
        (ANY, VMEM),
        buffers(1) + [pltpu.VMEM((span, width), dtype), pltpu.SemaphoreType.DMA((heads,))],
        share * heads,
    )

    def winner_part(g, part, second):
        return kernel_call(
            functools.partial(winner_kernel, g, ratio, block),
            (lengths, winners, weight, queries, own_output, own_mass, rival_keys, rival_values[g], part, second),
            [SMEM] * 2 + [VMEM] * 7 + [ANY],
            (second_shape, part_shape),
            (ANY, VMEM),
            buffers(1) + [pltpu.VMEM((span, ratio * HD), dtype), pltpu.SemaphoreType.DMA((ratio,))],
            share * ratio,
            {9: 0} if g else {},
        )

    def loser_part(index, second):
        g, low, high = cuts[index]
        return kernel_call(
            functools.partial(loser_kernel, g, low),
            (lengths, winners, pieces[index], companion_keys, companion_values, rival_keys, rival_values[g], second),
            [SMEM] * 2 + [VMEM] * 5 + [ANY],
            second_shape,
            ANY,
            buffers(2) + [pltpu.VMEM((half, (high - low) * HD), dtype), pltpu.SemaphoreType.DMA((high - low,))],
            share * (high - low),
            {7: 0},
        )

    part, second = first_part, first_part
    for g in range(groups):
        second, part = winner_part(g, part, second)
        if g < groups - 1:
            for index, cut in enumerate(cuts):
                second = loser_part(index, second) if cut[0] == g else second
    for index, cut in enumerate(cuts):
        second = loser_part(index, second) if cut[0] == groups - 1 else second

    cores = lax.axis_size("head")
    devices = lax.axis_size("cand") * cores
    diagonal = [(i, i ^ (cores + 1)) for i in range(devices)]
    score = jax.ShapeDtypeStruct((1,), jnp.float32)
    first_score, final_round_score = kernel_call(
        total_kernel,
        (
            lengths, winners, first_part, from_partner(first_part, "head", 0),
            part, from_partner(part, "head", 0), from_partner(part, "cand", 0), lax.ppermute(part, ("cand", "head"), diagonal),
        ),
        [SMEM] * 2 + [VMEM] * 6,
        (score, score),
        (SMEM, SMEM),
    )
    return first, second, first_score, final_round_score


def solution(mesh):
    in_specs = (
        P(("grp", "cand"), "head"),
        P(("grp", "cand"), "head"),
        P(("grp", "cand"), "head"),
        P("grp"),
        P("grp"),
        P("head"),
    )
    out_specs = (
        P(("grp", "cand"), "head"),
        P(("grp", "cand"), "head"),
        P(("grp", "cand")),
        P(("grp", "cand")),
    )
    return jax.shard_map(body, mesh=mesh, in_specs=in_specs, out_specs=out_specs, check_vma=False)
```

```python
import functools

import jax
import jax.numpy as jnp
from jax import lax
from jax.experimental import pallas as pl
from jax.experimental.pallas import tpu as pltpu
from jax.sharding import PartitionSpec as P

HD = 128
LANES = 128
LOG2E = 1.4426950408889634
FACTOR = HD ** (-0.5) * LOG2E
BARRED = -1e30
LAST_HEADS = 4
COST = 10
VMEM_LIMIT = 12 * 1024 * 1024
ANY = pl.BlockSpec(memory_space=pl.ANY)
HBM = pl.BlockSpec(memory_space=pltpu.HBM)
VMEM = pl.BlockSpec(memory_space=pltpu.VMEM)
SMEM = pl.BlockSpec(memory_space=pltpu.SMEM)


def from_partner(value, axis, stride):
    return lax.ppermute(value, axis, [(i, i ^ 1 << stride) for i in range(lax.axis_size(axis))])


class Place:
    def __init__(self, lengths_ref, winners_ref):
        device = lax.axis_index("cand")
        self.bit = device & 1
        pair = device >> 1
        self.winner = winners_ref[pair]
        self.won = self.bit == self.winner
        rival_pair = pair ^ 1
        self.own_valid = lengths_ref[device]
        self.partner_valid = lengths_ref[device ^ 1]
        self.rival_valid = lengths_ref[2 * rival_pair + winners_ref[rival_pair]]


def load_span(k_buf, v_buf, k_ref, v_ref, group, valid, start):
    span = k_ref.shape[0]
    k_columns = slice(group * HD, (group + 1) * HD)
    v_columns = k_columns if v_ref.shape[1] == k_ref.shape[1] else slice(0, HD)
    rows = slice(start, start + span)
    row = lax.broadcasted_iota(jnp.int32, (span, LANES), 0)
    first_lane = lax.broadcasted_iota(jnp.int32, (span, LANES), 1) == 0
    k_buf[rows, :HD] = k_ref[:, k_columns]
    k_buf[rows, HD:] = jnp.where(first_lane & (row >= valid), BARRED, 0.0).astype(k_buf.dtype)
    v_buf[rows, :HD] = v_ref[:, v_columns]
    v_buf[rows, HD:] = jnp.ones((span, LANES), v_buf.dtype)


def score_rows(q, k_buf):
    lane = lax.broadcasted_iota(jnp.int32, (q.shape[0], LANES), 1)
    one_lane = jnp.where(lane == 0, 1.0, 0.0).astype(q.dtype)
    wide_q = jnp.concatenate([q, one_lane], axis=1)
    return lax.dot_general(wide_q, k_buf[...], (((1,), (1,)), ((), ())), preferred_element_type=jnp.float32)


def weigh(scores, peak, v_buf):
    wide_peak = jnp.concatenate([peak] * (scores.shape[1] // LANES), axis=1)
    exps = jnp.exp2(scores * FACTOR - wide_peak).astype(v_buf.dtype)
    both = jnp.dot(exps, v_buf[...], preferred_element_type=jnp.float32)
    return both[:, :HD], both[:, HD:]


def peak_of(scores):
    peak = jnp.max(scores, axis=1, keepdims=True) * FACTOR
    return jnp.broadcast_to(peak, (scores.shape[0], LANES))


def finish(above, below, valid_rows, first_row, dtype):
    row = lax.broadcasted_iota(jnp.int32, above.shape, 0) + first_row
    return jnp.where(row < valid_rows, above / below, 0.0).astype(dtype)


def in_turn(works):
    scores = works[0][0]()
    for index, (_, finish_work) in enumerate(works):
        later = works[index + 1][0]() if index + 1 < len(works) else None
        finish_work(scores)
        scores = later


def own_kernel(ratio, block, cuts, lengths_ref, q_hbm, k_hbm, v_hbm, o_ref, sum_ref, peak_ref, *rest):
    piece_refs, (q_ref, k_ref, v_ref, k_buf, v_buf, sems) = rest[: len(cuts)], rest[len(cuts) :]
    groups = k_ref.shape[1] // HD
    copies = [pltpu.make_async_copy(k_hbm, k_ref, sems.at[0]), pltpu.make_async_copy(v_hbm, v_ref, sems.at[1])]
    for group in range(groups):
        columns = pl.ds(group * ratio * HD, ratio * HD)
        copies.append(pltpu.make_async_copy(q_hbm.at[:, columns], q_ref.at[:, columns], sems.at[2 + group]))
    for copy in copies:
        copy.start()
    copies[0].wait()
    copies[1].wait()
    device = lax.axis_index("cand")
    half = q_ref.shape[0] // 2
    sent = pl.ds(pl.multiple_of((1 - (device & 1)) * half, half), half)
    for group in range(groups):
        load_span(k_buf.at[group], v_buf.at[group], k_ref, v_ref, group, lengths_ref[device], 0)

    def score(rows, columns, group):
        if rows.start == 0 and columns.start == group * ratio * HD:
            copies[2 + group].wait()
        return score_rows(q_ref[rows, columns], k_buf.at[group])

    def weigh_own(rows, columns, group, scores):
        peak = peak_of(scores)
        o_ref[rows, columns], sum_ref[rows, columns] = weigh(scores, peak, v_buf.at[group])
        peak_ref[rows, columns] = peak

    works = []
    for head in range(groups * ratio):
        for start in range(0, q_ref.shape[0], block):
            place = (slice(start, start + block), slice(head * HD, (head + 1) * HD), head // ratio)
            works.append((functools.partial(score, *place), functools.partial(weigh_own, *place)))
    in_turn(works)
    for piece_ref, (low, high) in zip(piece_refs, cuts):
        piece_ref[...] = q_ref[sent, low * HD : high * HD]


def choose_kernel(lengths_ref, winners_ref, own_ref, companion_ref, *out_refs):
    place = Place(lengths_ref, winners_ref)
    for won, ref in ((True, own_ref), (False, companion_ref)):
        @pl.when(place.won == won)
        def _():
            start = 0
            for out_ref in out_refs:
                out_ref[...] = ref[:, start : start + out_ref.shape[1]]
                start += out_ref.shape[1]


def join_work(rows, first_row, columns, valid_rows, q_ref, own_refs, k_buf, v_buf, totals, keep_output):
    o_ref, sum_ref, peak_ref = own_refs

    def score():
        return score_rows(q_ref[rows, columns], k_buf)

    def join(scores):
        own_peak = peak_ref[rows, columns]
        peak = jnp.maximum(own_peak, peak_of(scores))
        above, below = weigh(scores, peak, v_buf)
        keep = jnp.exp2(own_peak - peak)
        above += o_ref[rows, columns] * keep
        below += sum_ref[rows, columns] * keep
        output = finish(above, below, valid_rows, first_row, q_ref.dtype)
        totals.append((columns, sum_rows(output)))
        keep_output(output)

    return score, join


def sum_rows(output):
    return jnp.sum(output.astype(jnp.float32).reshape(output.shape[0] // 8, 8, LANES), axis=0)


def weigh_totals(totals, weight_ref, valid):
    score = jnp.zeros((8, LANES), jnp.float32)
    for columns, total in totals:
        score += total * weight_ref[:, columns]
    return jnp.full((8, LANES), jnp.sum(score), jnp.float32) / valid.astype(jnp.float32)


def first_kernel(
    ratio, block, lengths_ref, weight_ref, q_ref, o_ref, sum_ref, peak_ref, k_ref, v_ref, out_ref, part_ref, k_buf, v_buf
):
    device = lax.axis_index("cand")
    span, heads = q_ref.shape[0], q_ref.shape[1] // HD
    valid = lengths_ref[device]
    for group in range(heads // ratio):
        load_span(k_buf.at[group], v_buf.at[group], k_ref, v_ref, group, lengths_ref[device ^ 1], 0)

    def keep(rows, columns, output):
        out_ref[rows, columns] = output

    works, totals = [], []
    for head in range(heads):
        for start in range(0, span, block):
            rows, columns = slice(start, start + block), slice(head * HD, (head + 1) * HD)
            works.append(
                join_work(
                    rows, start, columns, valid, q_ref, (o_ref, sum_ref, peak_ref), k_buf.at[head // ratio],
                    v_buf.at[head // ratio], totals, functools.partial(keep, rows, columns),
                )
            )
    in_turn(works)
    part_ref[...] = weigh_totals(totals, weight_ref, valid)


def lose_works(place, low, high, ratio, q_ref, k_buf, v_buf, totals, out_ref):
    def score(head):
        return score_rows(q_ref[:, (head - low) * HD : (head - low + 1) * HD], k_buf.at[head // ratio])

    def attend(head, scores):
        columns = slice(head * HD, (head + 1) * HD)
        above, below = weigh(scores, peak_of(scores), v_buf.at[head // ratio])
        first_row = place.bit * q_ref.shape[0]
        output = finish(above, below, place.partner_valid, first_row, out_ref.dtype)
        totals.append((columns, sum_rows(output)))
        out_ref[:, columns] = output

    return [(functools.partial(score, head), functools.partial(attend, head)) for head in range(low, high)]


def second_kernel(
    ratio, high, lengths_ref, winners_ref, weight_ref, q_ref, o_ref, sum_ref, peak_ref,
    ka_ref, va_ref, kb_ref, vb_ref, piece_ref, first_ref, out_ref, part_ref, k_buf, v_buf,
):
    place = Place(lengths_ref, winners_ref)
    half, span, heads = piece_ref.shape[0], q_ref.shape[0], q_ref.shape[1] // HD

    def give_part(part):
        row = lax.broadcasted_iota(jnp.int32, part.shape, 0)
        part_ref[...] = jnp.where(row == 0, part, first_ref[...])

    @pl.when(place.won)
    def _():
        for group in range(heads // ratio):
            load_span(k_buf.at[group, :span], v_buf.at[group, :span], kb_ref, vb_ref, group, place.rival_valid, 0)
        works, totals = [], []

        def keep(head, output):
            out_ref[:, head * HD : (head + 1) * HD] = output

        def work(head, start, keep_output):
            return join_work(
                pl.ds(start, half), start, slice(head * HD, (head + 1) * HD), place.own_valid, q_ref,
                (o_ref, sum_ref, peak_ref), k_buf.at[head // ratio, :span], v_buf.at[head // ratio, :span], totals,
                keep_output,
            )

        own_row = pl.multiple_of(place.bit * half, half)
        other_row = pl.multiple_of(half - own_row, half)
        works = [work(head, own_row, functools.partial(keep, head)) for head in range(heads)]
        works += [work(head, other_row, lambda output: None) for head in range(high, heads)]
        in_turn(works)
        give_part(weigh_totals(totals, weight_ref, place.own_valid))

    @pl.when(jnp.logical_not(place.won))
    def _():
        for group in range((high - 1) // ratio + 1):
            load_span(k_buf.at[group], v_buf.at[group], ka_ref, va_ref, group, place.partner_valid, 0)
            load_span(k_buf.at[group], v_buf.at[group], kb_ref, vb_ref, group, place.rival_valid, span)
        totals = []
        in_turn(lose_works(place, 0, high, ratio, piece_ref, k_buf, v_buf, totals, out_ref))
        give_part(weigh_totals(totals, weight_ref, place.partner_valid))


def last_kernel(
    ratio, low, lengths_ref, winners_ref, ka_ref, va_ref, kb_ref, vb_ref, piece_ref, first_ref, second_ref,
    first_out, second_out, k_buf, v_buf, out_buf, sems,
):
    place = Place(lengths_ref, winners_ref)
    heads, span = second_ref.shape[1] // HD, ka_ref.shape[0]
    before, after = pl.ds(0, low * HD), pl.ds(low * HD, (heads - low) * HD)
    first_copy = pltpu.make_async_copy(first_ref, first_out, sems.at[0])
    before_copy = pltpu.make_async_copy(second_ref.at[:, before], second_out.at[:, before], sems.at[1])
    won_copy = pltpu.make_async_copy(second_ref.at[:, after], second_out.at[:, after], sems.at[2])

    def lost_copy(head):
        columns = pl.ds(head * HD, HD)
        return pltpu.make_async_copy(out_buf.at[:, columns], second_out.at[:, columns], sems.at[3 + head - low])

    first_copy.start()
    before_copy.start()

    @pl.when(place.won)
    def _():
        won_copy.start()
        won_copy.wait()

    @pl.when(jnp.logical_not(place.won))
    def _():
        for group in range(low // ratio, heads // ratio):
            load_span(k_buf.at[group], v_buf.at[group], ka_ref, va_ref, group, place.partner_valid, 0)
            load_span(k_buf.at[group], v_buf.at[group], kb_ref, vb_ref, group, place.rival_valid, span)
        works = []
        for head, (score, attend) in zip(
            range(low, heads), lose_works(place, low, heads, ratio, piece_ref, k_buf, v_buf, [], out_buf)
        ):

            def attend_and_copy(scores, head=head, attend=attend):
                attend(scores)
                lost_copy(head).start()

            works.append((score, attend_and_copy))
        in_turn(works)
        for head in range(low, heads):
            lost_copy(head).wait()

    first_copy.wait()
    before_copy.wait()


def kernel_call(kernel, operands, in_specs, out_shape, out_specs, scratch=(), flops=0, aliases=None):
    return pl.pallas_call(
        kernel,
        out_shape=out_shape,
        in_specs=in_specs,
        out_specs=out_specs,
        scratch_shapes=scratch,
        input_output_aliases=aliases or {},
        compiler_params=pltpu.CompilerParams(vmem_limit_bytes=VMEM_LIMIT),
        cost_estimate=pl.CostEstimate(flops=COST * flops, bytes_accessed=COST * flops // 256, transcendentals=flops // 512),
    )(*operands)


def body(queries, keys, values, lengths, winners, score_weight):
    span, width = queries.shape
    half = span // 2
    heads = width // HD
    groups = keys.shape[1] // HD
    ratio = heads // groups
    block = min(span, 256)
    dtype = queries.dtype
    weight = score_weight.reshape(1, -1)
    share = 4 * span * span * HD
    part_shape = jax.ShapeDtypeStruct((8, LANES), jnp.float32)
    second_shape = jax.ShapeDtypeStruct((half, width), dtype)

    def buffers(spans):
        return [pltpu.VMEM((groups, spans * span, HD + LANES), dtype)] * 2

    companion_keys = from_partner(keys, "cand", 0)
    companion_values = from_partner(values, "cand", 0)

    middle = heads - LAST_HEADS
    cuts = [(0, middle), (middle, heads)]
    piece_shapes = tuple(jax.ShapeDtypeStruct((half, (high - low) * HD), dtype) for low, high in cuts)
    partial = jax.ShapeDtypeStruct((span, width), jnp.float32)
    *own, sent = kernel_call(
        functools.partial(own_kernel, ratio, block, cuts),
        (lengths, *[pltpu.with_memory_space_constraint(array, pltpu.HBM) for array in (queries, keys, values)]),
        [SMEM, HBM, HBM, HBM],
        (partial,) * 3 + piece_shapes,
        (VMEM,) * (3 + len(cuts)),
        [pltpu.VMEM(array.shape, dtype) for array in (queries, keys, values)]
        + buffers(1)
        + [pltpu.SemaphoreType.DMA((2 + groups,))],
        share * heads,
    )
    own, sent = own[:3], own[3:] + [sent]

    pieces = [from_partner(piece, "cand", 0) for piece in sent]

    def choose(own, companion, parts):
        shape = jax.ShapeDtypeStruct((span, own.shape[1] // parts), dtype)
        return kernel_call(
            choose_kernel, (lengths, winners, own, companion), [SMEM, SMEM, VMEM, VMEM], (shape,) * parts, (VMEM,) * parts
        )

    chosen_keys = choose(keys, companion_keys, 1)[0]
    rival_keys = from_partner(chosen_keys, "cand", 1)
    companion_values, _ = lax.optimization_barrier((companion_values, chosen_keys))
    rival_values = from_partner(choose(values, companion_values, 1)[0], "cand", 1)

    first_shape = jax.ShapeDtypeStruct((span, width), dtype)
    first, first_part = kernel_call(
        functools.partial(first_kernel, ratio, block),
        (lengths, weight, queries, *own, companion_keys, companion_values),
        [SMEM] + [VMEM] * 7,
        (first_shape, part_shape),
        (VMEM, VMEM),
        buffers(1),
        share * heads // 5,
    )
    second, part = kernel_call(
        functools.partial(second_kernel, ratio, middle),
        (
            lengths, winners, weight, queries, *own, companion_keys, companion_values, rival_keys, rival_values,
            pieces[0], first_part,
        ),
        [SMEM] * 2 + [VMEM] * 11,
        (second_shape, part_shape),
        (VMEM, VMEM),
        buffers(2),
        share * middle,
    )
    first, second = kernel_call(
        functools.partial(last_kernel, ratio, middle),
        (lengths, winners, companion_keys, companion_values, rival_keys, rival_values, pieces[1], first, second),
        [SMEM] * 2 + [VMEM] * 7,
        (first_shape, second_shape),
        (ANY, ANY),
        buffers(2) + [pltpu.VMEM((half, width), dtype), pltpu.SemaphoreType.DMA((3 + LAST_HEADS,))],
        share // 16,
    )

    cores = lax.axis_size("head")
    devices = lax.axis_size("cand") * cores
    diagonal = [(i, i ^ (cores + 1)) for i in range(devices)]
    beside = from_partner(part, "head", 0)
    across = from_partner(part, "cand", 0) + lax.ppermute(part, ("cand", "head"), diagonal)
    row = lax.broadcasted_iota(jnp.int32, part.shape, 0)
    sums = lax.optimization_barrier(part + beside + jnp.where(row == 0, across, 0.0))
    final_round_score, first_score = sums[0, :1], sums[1, :1]
    return first, second, first_score, final_round_score


def solution(mesh):
    in_specs = (
        P(("grp", "cand"), "head"),
        P(("grp", "cand"), "head"),
        P(("grp", "cand"), "head"),
        P("grp"),
        P("grp"),
        P("head"),
    )
    out_specs = (
        P(("grp", "cand"), "head"),
        P(("grp", "cand"), "head"),
        P(("grp", "cand")),
        P(("grp", "cand")),
    )
    return jax.shard_map(body, mesh=mesh, in_specs=in_specs, out_specs=out_specs, check_vma=False)
```

```python
import functools

import jax
import jax.numpy as jnp
from jax import lax
from jax.experimental import pallas as pl
from jax.experimental.pallas import tpu as pltpu
from jax.sharding import PartitionSpec as P

HD = 128
LANES = 128
LOG2E = 1.4426950408889634
FACTOR = HD ** (-0.5) * LOG2E
BARRED = -1e30
LAST_HEADS = 5
COST = 10
VMEM_LIMIT = 12 * 1024 * 1024
ANY = pl.BlockSpec(memory_space=pl.ANY)
HBM = pl.BlockSpec(memory_space=pltpu.HBM)
VMEM = pl.BlockSpec(memory_space=pltpu.VMEM)


def from_partner(value, axis, stride):
    return lax.ppermute(value, axis, [(i, i ^ 1 << stride) for i in range(lax.axis_size(axis))])


OWN_VALID, PARTNER_VALID, RIVAL_VALID, WON = range(4)


def gather_facts(lengths_ref, winners_ref):
    device = lax.axis_index("cand")
    pair = device >> 1
    rival_pair = pair ^ 1
    rival = 2 * rival_pair + winners_ref[rival_pair]
    won = jnp.where(winners_ref[pair] == (device & 1), 1, 0)
    row = lax.broadcasted_iota(jnp.int32, (8, LANES), 0)
    facts = jnp.zeros((8, LANES), jnp.int32)
    for index, number in enumerate((lengths_ref[device], lengths_ref[device ^ 1], lengths_ref[rival], won)):
        facts = jnp.where(row == index, number, facts)
    return facts.astype(jnp.float32)


def valid_of(facts_ref, index):
    return facts_ref[index : index + 1, :].astype(jnp.int32)


def has_won(facts_ref):
    return jnp.max(facts_ref[WON : WON + 1, :]) > 0.5


def load_span(k_buf, v_buf, k_ref, v_ref, group, valid, start):
    span = k_ref.shape[0]
    k_columns = slice(group * HD, (group + 1) * HD)
    v_columns = k_columns if v_ref.shape[1] == k_ref.shape[1] else slice(0, HD)
    rows = slice(start, start + span)
    row = lax.broadcasted_iota(jnp.int32, (span, LANES), 0)
    first_lane = lax.broadcasted_iota(jnp.int32, (span, LANES), 1) == 0
    k_buf[rows, :HD] = k_ref[:, k_columns]
    k_buf[rows, HD:] = jnp.where(first_lane & (row >= valid), BARRED, 0.0).astype(k_buf.dtype)
    v_buf[rows, :HD] = v_ref[:, v_columns]
    v_buf[rows, HD:] = jnp.ones((span, LANES), v_buf.dtype)


def score_rows(q, k_buf):
    lane = lax.broadcasted_iota(jnp.int32, (q.shape[0], LANES), 1)
    one_lane = jnp.where(lane == 0, 1.0, 0.0).astype(q.dtype)
    wide_q = jnp.concatenate([q, one_lane], axis=1)
    return lax.dot_general(wide_q, k_buf[...], (((1,), (1,)), ((), ())), preferred_element_type=jnp.float32)


def weigh(scores, peak, v_buf):
    wide_peak = jnp.concatenate([peak] * (scores.shape[1] // LANES), axis=1)
    exps = jnp.exp2(scores * FACTOR - wide_peak).astype(v_buf.dtype)
    both = jnp.dot(exps, v_buf[...], preferred_element_type=jnp.float32)
    return both[:, :HD], both[:, HD:]


def peak_of(scores):
    peak = jnp.max(scores, axis=1, keepdims=True) * FACTOR
    return jnp.broadcast_to(peak, (scores.shape[0], LANES))


def finish(above, below, valid_rows, first_row, dtype):
    row = lax.broadcasted_iota(jnp.int32, above.shape, 0) + first_row
    return jnp.where(row < valid_rows, above / below, 0.0).astype(dtype)


def in_turn(works):
    scores = works[0][0]()
    for index, (_, finish_work) in enumerate(works):
        later = works[index + 1][0]() if index + 1 < len(works) else None
        finish_work(scores)
        scores = later


def own_kernel(ratio, block, cuts, lengths_hbm, winners_hbm, q_hbm, k_hbm, v_hbm, o_ref, sum_ref, peak_ref, facts_ref, *rest):
    piece_refs, (q_ref, k_ref, v_ref, lengths_ref, winners_ref, k_buf, v_buf, sems) = rest[: len(cuts)], rest[len(cuts) :]
    groups = k_ref.shape[1] // HD
    lengths_copy = pltpu.make_async_copy(lengths_hbm, lengths_ref, sems.at[2 + groups])
    winners_copy = pltpu.make_async_copy(winners_hbm, winners_ref, sems.at[3 + groups])
    lengths_copy.start()
    winners_copy.start()
    copies = [pltpu.make_async_copy(k_hbm, k_ref, sems.at[0]), pltpu.make_async_copy(v_hbm, v_ref, sems.at[1])]
    for group in range(groups):
        columns = pl.ds(group * ratio * HD, ratio * HD)
        copies.append(pltpu.make_async_copy(q_hbm.at[:, columns], q_ref.at[:, columns], sems.at[2 + group]))
    for copy in copies:
        copy.start()
    lengths_copy.wait()
    winners_copy.wait()
    facts_ref[...] = gather_facts(lengths_ref, winners_ref)
    copies[0].wait()
    copies[1].wait()
    device = lax.axis_index("cand")
    half = q_ref.shape[0] // 2
    sent = pl.ds(pl.multiple_of((1 - (device & 1)) * half, half), half)
    for group in range(groups):
        load_span(k_buf.at[group], v_buf.at[group], k_ref, v_ref, group, valid_of(facts_ref, OWN_VALID), 0)

    def score(rows, columns, group):
        if rows.start == 0 and columns.start == group * ratio * HD:
            copies[2 + group].wait()
        return score_rows(q_ref[rows, columns], k_buf.at[group])

    def weigh_own(rows, columns, group, scores):
        peak = peak_of(scores)
        o_ref[rows, columns], sum_ref[rows, columns] = weigh(scores, peak, v_buf.at[group])
        peak_ref[rows, columns] = peak

    works = []
    for head in range(groups * ratio):
        for start in range(0, q_ref.shape[0], block):
            place = (slice(start, start + block), slice(head * HD, (head + 1) * HD), head // ratio)
            works.append((functools.partial(score, *place), functools.partial(weigh_own, *place)))
    in_turn(works)
    for piece_ref, (low, high) in zip(piece_refs, cuts):
        piece_ref[...] = q_ref[sent, low * HD : high * HD]


def choose_kernel(facts_ref, own_ref, companion_ref, out_ref):
    won = has_won(facts_ref)

    @pl.when(won)
    def _():
        out_ref[...] = own_ref[...]

    @pl.when(jnp.logical_not(won))
    def _():
        out_ref[...] = companion_ref[...]


def join_work(rows, first_row, columns, valid_rows, q_ref, own_refs, k_buf, v_buf, totals, keep_output):
    o_ref, sum_ref, peak_ref = own_refs

    def score():
        return score_rows(q_ref[rows, columns], k_buf)

    def join(scores):
        own_peak = peak_ref[rows, columns]
        peak = jnp.maximum(own_peak, peak_of(scores))
        above, below = weigh(scores, peak, v_buf)
        keep = jnp.exp2(own_peak - peak)
        above += o_ref[rows, columns] * keep
        below += sum_ref[rows, columns] * keep
        output = finish(above, below, valid_rows, first_row, q_ref.dtype)
        totals.append((columns, sum_rows(output)))
        keep_output(output)

    return score, join


def sum_rows(output):
    return jnp.sum(output.astype(jnp.float32).reshape(output.shape[0] // 8, 8, LANES), axis=0)


def weigh_totals(totals, weight_ref, facts_ref, index):
    valid = facts_ref[index : index + 1, :]
    score = jnp.zeros((8, LANES), jnp.float32)
    for columns, total in totals:
        score += total * weight_ref[:, columns]
    return jnp.full((8, LANES), jnp.sum(score), jnp.float32) / valid


def first_kernel(
    ratio, block, facts_ref, weight_ref, q_ref, o_ref, sum_ref, peak_ref, k_ref, v_ref, out_ref, part_ref, k_buf, v_buf
):
    span, heads = q_ref.shape[0], q_ref.shape[1] // HD
    valid = valid_of(facts_ref, OWN_VALID)
    for group in range(heads // ratio):
        load_span(k_buf.at[group], v_buf.at[group], k_ref, v_ref, group, valid_of(facts_ref, PARTNER_VALID), 0)

    def keep(rows, columns, output):
        out_ref[rows, columns] = output

    works, totals = [], []
    for head in range(heads):
        for start in range(0, span, block):
            rows, columns = slice(start, start + block), slice(head * HD, (head + 1) * HD)
            works.append(
                join_work(
                    rows, start, columns, valid, q_ref, (o_ref, sum_ref, peak_ref), k_buf.at[head // ratio],
                    v_buf.at[head // ratio], totals, functools.partial(keep, rows, columns),
                )
            )
    in_turn(works)
    part_ref[...] = weigh_totals(totals, weight_ref, facts_ref, OWN_VALID)


def lose_works(facts_ref, low, high, ratio, q_ref, k_buf, v_buf, totals, out_ref):
    def score(head):
        return score_rows(q_ref[:, (head - low) * HD : (head - low + 1) * HD], k_buf.at[head // ratio])

    def attend(head, scores):
        columns = slice(head * HD, (head + 1) * HD)
        above, below = weigh(scores, peak_of(scores), v_buf.at[head // ratio])
        first_row = (lax.axis_index("cand") & 1) * q_ref.shape[0]
        output = finish(above, below, valid_of(facts_ref, PARTNER_VALID), first_row, out_ref.dtype)
        totals.append((columns, sum_rows(output)))
        out_ref[:, columns] = output

    return [(functools.partial(score, head), functools.partial(attend, head)) for head in range(low, high)]


def second_kernel(
    ratio, high, facts_ref, weight_ref, q_ref, o_ref, sum_ref, peak_ref,
    ka_ref, va_ref, kb_ref, vb_ref, piece_ref, first_ref, out_ref, part_ref, k_buf, v_buf,
):
    won = has_won(facts_ref)
    half, span, heads = piece_ref.shape[0], q_ref.shape[0], q_ref.shape[1] // HD

    def give_part(part):
        row = lax.broadcasted_iota(jnp.int32, part.shape, 0)
        part_ref[...] = jnp.where(row == 0, part, first_ref[...])

    @pl.when(won)
    def _():
        for group in range(heads // ratio):
            load_span(k_buf.at[group, :span], v_buf.at[group, :span], kb_ref, vb_ref, group, valid_of(facts_ref, RIVAL_VALID), 0)
        works, totals = [], []

        def keep(head, output):
            out_ref[:, head * HD : (head + 1) * HD] = output

        def work(head, start, keep_output):
            return join_work(
                pl.ds(start, half), start, slice(head * HD, (head + 1) * HD), valid_of(facts_ref, OWN_VALID), q_ref,
                (o_ref, sum_ref, peak_ref), k_buf.at[head // ratio, :span], v_buf.at[head // ratio, :span], totals,
                keep_output,
            )

        own_row = pl.multiple_of((lax.axis_index("cand") & 1) * half, half)
        other_row = pl.multiple_of(half - own_row, half)
        works = [work(head, own_row, functools.partial(keep, head)) for head in range(heads)]
        works += [work(head, other_row, lambda output: None) for head in range(high, heads)]
        in_turn(works)
        give_part(weigh_totals(totals, weight_ref, facts_ref, OWN_VALID))

    @pl.when(jnp.logical_not(won))
    def _():
        for group in range((high - 1) // ratio + 1):
            load_span(k_buf.at[group], v_buf.at[group], ka_ref, va_ref, group, valid_of(facts_ref, PARTNER_VALID), 0)
            load_span(k_buf.at[group], v_buf.at[group], kb_ref, vb_ref, group, valid_of(facts_ref, RIVAL_VALID), span)
        totals = []
        in_turn(lose_works(facts_ref, 0, high, ratio, piece_ref, k_buf, v_buf, totals, out_ref))
        give_part(weigh_totals(totals, weight_ref, facts_ref, PARTNER_VALID))


def last_kernel(
    ratio, low, facts_ref, ka_ref, va_ref, kb_ref, vb_ref, piece_ref, first_ref, second_ref,
    first_out, second_out, k_buf, v_buf, out_buf, sems,
):
    won = has_won(facts_ref)
    heads, span = second_ref.shape[1] // HD, ka_ref.shape[0]
    before, after = pl.ds(0, low * HD), pl.ds(low * HD, (heads - low) * HD)
    first_copy = pltpu.make_async_copy(first_ref, first_out, sems.at[0])
    before_copy = pltpu.make_async_copy(second_ref.at[:, before], second_out.at[:, before], sems.at[1])
    won_copy = pltpu.make_async_copy(second_ref.at[:, after], second_out.at[:, after], sems.at[2])

    def lost_copy(head):
        columns = pl.ds(head * HD, HD)
        return pltpu.make_async_copy(out_buf.at[:, columns], second_out.at[:, columns], sems.at[3 + head - low])

    first_copy.start()
    before_copy.start()

    @pl.when(won)
    def _():
        won_copy.start()
        won_copy.wait()

    @pl.when(jnp.logical_not(won))
    def _():
        for group in range(low // ratio, heads // ratio):
            load_span(k_buf.at[group], v_buf.at[group], ka_ref, va_ref, group, valid_of(facts_ref, PARTNER_VALID), 0)
            load_span(k_buf.at[group], v_buf.at[group], kb_ref, vb_ref, group, valid_of(facts_ref, RIVAL_VALID), span)
        works = []
        for head, (score, attend) in zip(
            range(low, heads), lose_works(facts_ref, low, heads, ratio, piece_ref, k_buf, v_buf, [], out_buf)
        ):

            def attend_and_copy(scores, head=head, attend=attend):
                attend(scores)
                lost_copy(head).start()

            works.append((score, attend_and_copy))
        in_turn(works)
        for head in range(low, heads):
            lost_copy(head).wait()

    first_copy.wait()
    before_copy.wait()


def kernel_call(kernel, operands, in_specs, out_shape, out_specs, scratch=(), flops=0, aliases=None):
    return pl.pallas_call(
        kernel,
        out_shape=out_shape,
        in_specs=in_specs,
        out_specs=out_specs,
        scratch_shapes=scratch,
        input_output_aliases=aliases or {},
        compiler_params=pltpu.CompilerParams(vmem_limit_bytes=VMEM_LIMIT),
        cost_estimate=pl.CostEstimate(flops=COST * flops, bytes_accessed=COST * flops // 256, transcendentals=flops // 512),
    )(*operands)


def body(queries, keys, values, lengths, winners, score_weight):
    span, width = queries.shape
    half = span // 2
    heads = width // HD
    groups = keys.shape[1] // HD
    ratio = heads // groups
    block = min(span, 256)
    dtype = queries.dtype
    weight = score_weight.reshape(1, -1)
    share = 4 * span * span * HD
    part_shape = jax.ShapeDtypeStruct((8, LANES), jnp.float32)
    second_shape = jax.ShapeDtypeStruct((half, width), dtype)

    def buffers(spans):
        return [pltpu.VMEM((groups, spans * span, HD + LANES), dtype)] * 2

    companion_keys = from_partner(keys, "cand", 0)
    companion_values = from_partner(values, "cand", 0)

    middle = heads - LAST_HEADS
    cuts = [(0, middle), (middle, heads)]
    piece_shapes = tuple(jax.ShapeDtypeStruct((half, (high - low) * HD), dtype) for low, high in cuts)
    partial = jax.ShapeDtypeStruct((span, width), jnp.float32)
    *own, sent = kernel_call(
        functools.partial(own_kernel, ratio, block, cuts),
        [pltpu.with_memory_space_constraint(array, pltpu.HBM) for array in (lengths, winners, queries, keys, values)],
        [HBM] * 5,
        (partial,) * 3 + (part_shape,) + piece_shapes,
        (VMEM,) * (4 + len(cuts)),
        [pltpu.VMEM(array.shape, dtype) for array in (queries, keys, values)]
        + [pltpu.SMEM(array.shape, array.dtype) for array in (lengths, winners)]
        + buffers(1)
        + [pltpu.SemaphoreType.DMA((4 + groups,))],
        share * heads,
    )
    own, facts, sent = own[:3], own[3], own[4:] + [sent]

    pieces = [from_partner(piece, "cand", 0) for piece in sent]

    def choose(own, companion):
        shape = jax.ShapeDtypeStruct(own.shape, dtype)
        return kernel_call(choose_kernel, (facts, own, companion), [VMEM] * 3, shape, VMEM)

    chosen_keys = choose(keys, companion_keys)
    rival_keys = from_partner(chosen_keys, "cand", 1)
    companion_values, _ = lax.optimization_barrier((companion_values, chosen_keys))
    rival_values = from_partner(choose(values, companion_values), "cand", 1)

    first_shape = jax.ShapeDtypeStruct((span, width), dtype)
    first, first_part = kernel_call(
        functools.partial(first_kernel, ratio, block),
        (facts, weight, queries, *own, companion_keys, companion_values),
        [VMEM] * 8,
        (first_shape, part_shape),
        (VMEM, VMEM),
        buffers(1),
        share * heads // 6,
    )
    second, part = kernel_call(
        functools.partial(second_kernel, ratio, middle),
        (
            facts, weight, queries, *own, companion_keys, companion_values, rival_keys, rival_values,
            pieces[0], first_part,
        ),
        [VMEM] * 12,
        (second_shape, part_shape),
        (VMEM, VMEM),
        buffers(2),
        share * middle,
    )
    first, second = kernel_call(
        functools.partial(last_kernel, ratio, middle),
        (facts, companion_keys, companion_values, rival_keys, rival_values, pieces[1], first, second),
        [VMEM] * 8,
        (first_shape, second_shape),
        (ANY, ANY),
        buffers(2) + [pltpu.VMEM((half, width), dtype), pltpu.SemaphoreType.DMA((3 + LAST_HEADS,))],
        share // 16,
    )

    cores = lax.axis_size("head")
    devices = lax.axis_size("cand") * cores
    diagonal = [(i, i ^ (cores + 1)) for i in range(devices)]
    beside = from_partner(part, "head", 0)
    across = from_partner(part, "cand", 0) + lax.ppermute(part, ("cand", "head"), diagonal)
    row = lax.broadcasted_iota(jnp.int32, part.shape, 0)
    sums = lax.optimization_barrier(part + beside + jnp.where(row == 0, across, 0.0))
    final_round_score, first_score = sums[0, :1], sums[1, :1]
    return first, second, first_score, final_round_score


def solution(mesh):
    in_specs = (
        P(("grp", "cand"), "head"),
        P(("grp", "cand"), "head"),
        P(("grp", "cand"), "head"),
        P("grp"),
        P("grp"),
        P("head"),
    )
    out_specs = (
        P(("grp", "cand"), "head"),
        P(("grp", "cand"), "head"),
        P(("grp", "cand")),
        P(("grp", "cand")),
    )
    return jax.shard_map(body, mesh=mesh, in_specs=in_specs, out_specs=out_specs, check_vma=False)
```

```python
import functools

import jax
import jax.numpy as jnp
from jax import lax
from jax.experimental import pallas as pl
from jax.experimental.pallas import tpu as pltpu
from jax.sharding import PartitionSpec as P

HD = 128
LANES = 128
LOG2E = 1.4426950408889634
FACTOR = HD ** (-0.5) * LOG2E
BARRED = -1e30
LAST_HEADS = 5
TAIL_HEADS = 3
COST = 10
VMEM_LIMIT = 12 * 1024 * 1024
ANY = pl.BlockSpec(memory_space=pl.ANY)
HBM = pl.BlockSpec(memory_space=pltpu.HBM)
VMEM = pl.BlockSpec(memory_space=pltpu.VMEM)


def from_partner(value, axis, stride):
    return lax.ppermute(value, axis, [(i, i ^ 1 << stride) for i in range(lax.axis_size(axis))])


OWN_VALID, PARTNER_VALID, RIVAL_VALID, WON = range(4)


def gather_facts(lengths_ref, winners_ref):
    device = lax.axis_index("cand")
    pair = device >> 1
    rival_pair = pair ^ 1
    rival = 2 * rival_pair + winners_ref[rival_pair]
    won = jnp.where(winners_ref[pair] == (device & 1), 1, 0)
    row = lax.broadcasted_iota(jnp.int32, (8, LANES), 0)
    facts = jnp.zeros((8, LANES), jnp.int32)
    for index, number in enumerate((lengths_ref[device], lengths_ref[device ^ 1], lengths_ref[rival], won)):
        facts = jnp.where(row == index, number, facts)
    return facts.astype(jnp.float32)


def valid_of(facts_ref, index):
    return facts_ref[index : index + 1, :].astype(jnp.int32)


def has_won(facts_ref):
    return jnp.max(facts_ref[WON : WON + 1, :]) > 0.5


def load_span(k_buf, v_buf, k_ref, v_ref, group, valid, start):
    span = k_ref.shape[0]
    k_columns = slice(group * HD, (group + 1) * HD)
    v_columns = k_columns if v_ref.shape[1] == k_ref.shape[1] else slice(0, HD)
    rows = slice(start, start + span)
    row = lax.broadcasted_iota(jnp.int32, (span, LANES), 0)
    first_lane = lax.broadcasted_iota(jnp.int32, (span, LANES), 1) == 0
    k_buf[rows, :HD] = k_ref[:, k_columns]
    k_buf[rows, HD:] = jnp.where(first_lane & (row >= valid), BARRED, 0.0).astype(k_buf.dtype)
    v_buf[rows, :HD] = v_ref[:, v_columns]
    v_buf[rows, HD:] = jnp.ones((span, LANES), v_buf.dtype)


def score_rows(q, k_buf):
    lane = lax.broadcasted_iota(jnp.int32, (q.shape[0], LANES), 1)
    one_lane = jnp.where(lane == 0, 1.0, 0.0).astype(q.dtype)
    wide_q = jnp.concatenate([q, one_lane], axis=1)
    return lax.dot_general(wide_q, k_buf[...], (((1,), (1,)), ((), ())), preferred_element_type=jnp.float32)


def weigh(scores, peak, v_buf):
    wide_peak = jnp.concatenate([peak] * (scores.shape[1] // LANES), axis=1)
    exps = jnp.exp2(scores * FACTOR - wide_peak).astype(v_buf.dtype)
    both = jnp.dot(exps, v_buf[...], preferred_element_type=jnp.float32)
    return both[:, :HD], both[:, HD:]


def peak_of(scores):
    peak = jnp.max(scores, axis=1, keepdims=True) * FACTOR
    return jnp.broadcast_to(peak, (scores.shape[0], LANES))


def finish(above, below, valid_rows, first_row, dtype):
    row = lax.broadcasted_iota(jnp.int32, above.shape, 0) + first_row
    return jnp.where(row < valid_rows, above / below, 0.0).astype(dtype)


def in_turn(works):
    scores = works[0][0]()
    for index, (_, finish_work) in enumerate(works):
        later = works[index + 1][0]() if index + 1 < len(works) else None
        finish_work(scores)
        scores = later


def own_kernel(ratio, block, cuts, lengths_hbm, winners_hbm, q_hbm, k_hbm, v_hbm, o_ref, sum_ref, peak_ref, facts_ref, *rest):
    piece_refs, (q_ref, k_ref, v_ref, lengths_ref, winners_ref, k_buf, v_buf, sems) = rest[: len(cuts)], rest[len(cuts) :]
    groups = k_ref.shape[1] // HD
    lengths_copy = pltpu.make_async_copy(lengths_hbm, lengths_ref, sems.at[2 + groups])
    winners_copy = pltpu.make_async_copy(winners_hbm, winners_ref, sems.at[3 + groups])
    lengths_copy.start()
    winners_copy.start()
    copies = [pltpu.make_async_copy(k_hbm, k_ref, sems.at[0]), pltpu.make_async_copy(v_hbm, v_ref, sems.at[1])]
    for group in range(groups):
        columns = pl.ds(group * ratio * HD, ratio * HD)
        copies.append(pltpu.make_async_copy(q_hbm.at[:, columns], q_ref.at[:, columns], sems.at[2 + group]))
    for copy in copies:
        copy.start()
    lengths_copy.wait()
    winners_copy.wait()
    facts_ref[...] = gather_facts(lengths_ref, winners_ref)
    copies[0].wait()
    copies[1].wait()
    device = lax.axis_index("cand")
    half = q_ref.shape[0] // 2
    sent = pl.ds(pl.multiple_of((1 - (device & 1)) * half, half), half)
    for group in range(groups):
        load_span(k_buf.at[group], v_buf.at[group], k_ref, v_ref, group, valid_of(facts_ref, OWN_VALID), 0)

    def score(rows, columns, group):
        if rows.start == 0 and columns.start == group * ratio * HD:
            copies[2 + group].wait()
        return score_rows(q_ref[rows, columns], k_buf.at[group])

    def weigh_own(rows, columns, group, scores):
        peak = peak_of(scores)
        o_ref[rows, columns], sum_ref[rows, columns] = weigh(scores, peak, v_buf.at[group])
        peak_ref[rows, columns] = peak

    works = []
    for head in range(groups * ratio):
        for start in range(0, q_ref.shape[0], block):
            place = (slice(start, start + block), slice(head * HD, (head + 1) * HD), head // ratio)
            works.append((functools.partial(score, *place), functools.partial(weigh_own, *place)))
    in_turn(works)
    for piece_ref, (low, high) in zip(piece_refs, cuts):
        piece_ref[...] = q_ref[sent, low * HD : high * HD]


def choose_kernel(facts_ref, own_ref, companion_ref, out_ref):
    won = has_won(facts_ref)

    @pl.when(won)
    def _():
        out_ref[...] = own_ref[...]

    @pl.when(jnp.logical_not(won))
    def _():
        out_ref[...] = companion_ref[...]


def join_work(rows, first_row, columns, valid_rows, q_ref, own_refs, k_buf, v_buf, totals, keep_output):
    o_ref, sum_ref, peak_ref = own_refs

    def score():
        return score_rows(q_ref[rows, columns], k_buf)

    def join(scores):
        own_peak = peak_ref[rows, columns]
        peak = jnp.maximum(own_peak, peak_of(scores))
        above, below = weigh(scores, peak, v_buf)
        keep = jnp.exp2(own_peak - peak)
        above += o_ref[rows, columns] * keep
        below += sum_ref[rows, columns] * keep
        output = finish(above, below, valid_rows, first_row, q_ref.dtype)
        totals.append((columns, sum_rows(output)))
        keep_output(output)

    return score, join


def sum_rows(output):
    return jnp.sum(output.astype(jnp.float32).reshape(output.shape[0] // 8, 8, LANES), axis=0)


def weigh_totals(totals, weight_ref, facts_ref, index):
    valid = facts_ref[index : index + 1, :]
    score = jnp.zeros((8, LANES), jnp.float32)
    for columns, total in totals:
        score += total * weight_ref[:, columns]
    return jnp.full((8, LANES), jnp.sum(score), jnp.float32) / valid


def first_kernel(
    ratio, block, facts_ref, weight_ref, q_ref, o_ref, sum_ref, peak_ref, k_ref, v_ref, out_ref, part_ref, k_buf, v_buf
):
    span, heads = q_ref.shape[0], q_ref.shape[1] // HD
    valid = valid_of(facts_ref, OWN_VALID)
    for group in range(heads // ratio):
        load_span(k_buf.at[group], v_buf.at[group], k_ref, v_ref, group, valid_of(facts_ref, PARTNER_VALID), 0)

    def keep(rows, columns, output):
        out_ref[rows, columns] = output

    works, totals = [], []
    for head in range(heads):
        for start in range(0, span, block):
            rows, columns = slice(start, start + block), slice(head * HD, (head + 1) * HD)
            works.append(
                join_work(
                    rows, start, columns, valid, q_ref, (o_ref, sum_ref, peak_ref), k_buf.at[head // ratio],
                    v_buf.at[head // ratio], totals, functools.partial(keep, rows, columns),
                )
            )
    in_turn(works)
    part_ref[...] = weigh_totals(totals, weight_ref, facts_ref, OWN_VALID)


def lose_works(facts_ref, low, high, ratio, q_ref, k_buf, v_buf, totals, out_ref, then=None):
    half, span = q_ref.shape[0], k_buf.shape[1] // 2
    chunks, head = [], low
    while head < high:
        after = min(head + 2, high, (head // ratio + 1) * ratio)
        chunks.append(range(head, after))
        head = after

    def score(chunk):
        rows = jnp.concatenate([q_ref[:, (head - low) * HD : (head - low + 1) * HD] for head in chunk], axis=0)
        k_wide = k_buf.at[chunk[0] // ratio]
        return [score_rows(rows, k_wide.at[start : start + span]) for start in (0, span)]

    def attend(chunk, scores):
        v_wide = v_buf.at[chunk[0] // ratio]
        peak = jnp.maximum(*(jnp.max(each, axis=1, keepdims=True) for each in scores))
        both = 0.0
        for each, start in zip(scores, (0, span)):
            exps = jnp.exp2((each - peak) * FACTOR).astype(v_wide.dtype)
            both += jnp.dot(exps, v_wide[start : start + span], preferred_element_type=jnp.float32)
        first_row = (lax.axis_index("cand") & 1) * half
        for index, head in enumerate(chunk):
            columns = slice(head * HD, (head + 1) * HD)
            rows = both[index * half : (index + 1) * half]
            output = finish(rows[:, :HD], rows[:, HD:], valid_of(facts_ref, PARTNER_VALID), first_row, out_ref.dtype)
            totals.append((columns, sum_rows(output)))
            out_ref[:, columns] = output
            if then is not None:
                then(head)

    return [(functools.partial(score, chunk), functools.partial(attend, chunk)) for chunk in chunks]


def give_part(part_ref, part, first_ref):
    row = lax.broadcasted_iota(jnp.int32, part.shape, 0)
    part_ref[...] = jnp.where(row == 0, part, first_ref[...])


def win_kernel(
    ratio, low, facts_ref, weight_ref, q_ref, o_ref, sum_ref, peak_ref, k_ref, v_ref, first_ref, out_ref, part_ref, k_buf, v_buf
):
    half, heads = out_ref.shape[0], q_ref.shape[1] // HD

    @pl.when(has_won(facts_ref))
    def _():
        for group in range(heads // ratio):
            load_span(k_buf.at[group], v_buf.at[group], k_ref, v_ref, group, valid_of(facts_ref, RIVAL_VALID), 0)
        totals = []

        def keep(head, output):
            out_ref[:, head * HD : (head + 1) * HD] = output

        def work(head, start, keep_output):
            return join_work(
                pl.ds(start, half), start, slice(head * HD, (head + 1) * HD), valid_of(facts_ref, OWN_VALID), q_ref,
                (o_ref, sum_ref, peak_ref), k_buf.at[head // ratio], v_buf.at[head // ratio], totals, keep_output,
            )

        own_row = pl.multiple_of((lax.axis_index("cand") & 1) * half, half)
        other_row = pl.multiple_of(half - own_row, half)
        works = [work(head, own_row, functools.partial(keep, head)) for head in range(heads)]
        works += [work(head, other_row, lambda output: None) for head in range(low, heads)]
        in_turn(works)
        give_part(part_ref, weigh_totals(totals, weight_ref, facts_ref, OWN_VALID), first_ref)


def lose_kernel(
    ratio, high, facts_ref, weight_ref, ka_ref, va_ref, kb_ref, vb_ref, piece_ref, first_ref, second_ref, won_part_ref,
    out_ref, part_ref, k_wide, v_wide,
):
    span = ka_ref.shape[0]

    @pl.when(jnp.logical_not(has_won(facts_ref)))
    def _():
        for group in range(k_wide.shape[0]):
            own_k, own_v = k_wide.at[group], v_wide.at[group]
            load_span(own_k, own_v, ka_ref, va_ref, group, valid_of(facts_ref, PARTNER_VALID), 0)
            load_span(own_k, own_v, kb_ref, vb_ref, group, valid_of(facts_ref, RIVAL_VALID), span)
        totals = []
        in_turn(lose_works(facts_ref, 0, high, ratio, piece_ref, k_wide, v_wide, totals, out_ref))
        give_part(part_ref, weigh_totals(totals, weight_ref, facts_ref, PARTNER_VALID), first_ref)


def last_kernel(
    ratio, low, facts_ref, k_wide, v_wide, piece_ref, first_ref, second_ref, first_out, second_out, out_ref, sems
):
    won = has_won(facts_ref)
    heads = second_ref.shape[1] // HD
    before, after = pl.ds(0, low * HD), pl.ds(low * HD, (heads - low) * HD)
    first_copy = pltpu.make_async_copy(first_ref, first_out, sems.at[0])
    before_copy = pltpu.make_async_copy(second_ref.at[:, before], second_out.at[:, before], sems.at[1])
    won_copy = pltpu.make_async_copy(second_ref.at[:, after], second_out.at[:, after], sems.at[2])

    def lost_copy(head):
        columns = pl.ds(head * HD, HD)
        return pltpu.make_async_copy(out_ref.at[:, columns], second_out.at[:, columns], sems.at[3 + head - low])

    first_copy.start()
    before_copy.start()

    @pl.when(won)
    def _():
        won_copy.start()
        won_copy.wait()

    @pl.when(jnp.logical_not(won))
    def _():
        def copy_out(head):
            if head < heads - TAIL_HEADS:
                lost_copy(head).start()

        in_turn(lose_works(facts_ref, low, heads, ratio, piece_ref, k_wide, v_wide, [], out_ref, copy_out))
        for head in range(low, heads - TAIL_HEADS):
            lost_copy(head).wait()

    first_copy.wait()
    before_copy.wait()


def final_kernel(
    facts_ref, part_ref, beside_ref, across_ref, diagonal_ref, lost_ref, _, second_out, first_score, final_score,
    first_buf, final_buf, sems,
):
    won = has_won(facts_ref)
    width = TAIL_HEADS * HD
    columns = pl.ds(second_out.shape[1] - width, width)
    tail_copy = pltpu.make_async_copy(lost_ref.at[:, columns], second_out.at[:, columns], sems.at[2])

    @pl.when(jnp.logical_not(won))
    def _():
        tail_copy.start()

    beside = part_ref[...] + beside_ref[...]
    total = beside + (across_ref[...] + diagonal_ref[...])
    score_copies = []
    scores = ((beside[1:2, :], first_buf, first_score), (total[0:1, :], final_buf, final_score))
    for index, (score, buf, out) in enumerate(scores):
        buf[0] = jnp.max(score)
        copy = pltpu.make_async_copy(buf, out, sems.at[index])
        copy.start()
        score_copies.append(copy)
    for copy in score_copies:
        copy.wait()

    @pl.when(jnp.logical_not(won))
    def _():
        tail_copy.wait()


def kernel_call(kernel, operands, in_specs, out_shape, out_specs, scratch=(), flops=0, aliases=None):
    return pl.pallas_call(
        kernel,
        out_shape=out_shape,
        in_specs=in_specs,
        out_specs=out_specs,
        scratch_shapes=scratch,
        input_output_aliases=aliases or {},
        compiler_params=pltpu.CompilerParams(vmem_limit_bytes=VMEM_LIMIT),
        cost_estimate=pl.CostEstimate(flops=COST * flops, bytes_accessed=COST * flops // 256, transcendentals=flops // 512),
    )(*operands)


def body(queries, keys, values, lengths, winners, score_weight):
    span, width = queries.shape
    half = span // 2
    heads = width // HD
    groups = keys.shape[1] // HD
    ratio = heads // groups
    block = min(span, 256)
    dtype = queries.dtype
    weight = score_weight.reshape(1, -1)
    share = 4 * span * span * HD
    part_shape = jax.ShapeDtypeStruct((8, LANES), jnp.float32)
    second_shape = jax.ShapeDtypeStruct((half, width), dtype)

    def buffers(spans):
        return [pltpu.VMEM((groups, spans * span, HD + LANES), dtype)] * 2

    companion_keys = from_partner(keys, "cand", 0)
    companion_values = from_partner(values, "cand", 0)

    middle = heads - LAST_HEADS
    cuts = [(0, middle), (middle, heads)]
    piece_shapes = tuple(jax.ShapeDtypeStruct((half, (high - low) * HD), dtype) for low, high in cuts)
    partial = jax.ShapeDtypeStruct((span, width), jnp.float32)
    *own, sent = kernel_call(
        functools.partial(own_kernel, ratio, block, cuts),
        [pltpu.with_memory_space_constraint(array, pltpu.HBM) for array in (lengths, winners, queries, keys, values)],
        [HBM] * 5,
        (partial,) * 3 + (part_shape,) + piece_shapes,
        (VMEM,) * (4 + len(cuts)),
        [pltpu.VMEM(array.shape, dtype) for array in (queries, keys, values)]
        + [pltpu.SMEM(array.shape, array.dtype) for array in (lengths, winners)]
        + buffers(1)
        + [pltpu.SemaphoreType.DMA((4 + groups,))],
        share * heads,
    )
    own, facts, sent = own[:3], own[3], own[4:] + [sent]

    pieces = [from_partner(piece, "cand", 0) for piece in sent]

    def choose(own, companion):
        shape = jax.ShapeDtypeStruct(own.shape, dtype)
        return kernel_call(choose_kernel, (facts, own, companion), [VMEM] * 3, shape, VMEM)

    chosen_keys = choose(keys, companion_keys)
    rival_keys = from_partner(chosen_keys, "cand", 1)
    companion_values, _ = lax.optimization_barrier((companion_values, chosen_keys))
    rival_values = from_partner(choose(values, companion_values), "cand", 1)

    first_shape = jax.ShapeDtypeStruct((span, width), dtype)
    first, first_part = kernel_call(
        functools.partial(first_kernel, ratio, block),
        (facts, weight, queries, *own, companion_keys, companion_values),
        [VMEM] * 8,
        (first_shape, part_shape),
        (VMEM, VMEM),
        buffers(1),
        share * heads // 2,
    )
    second, part = kernel_call(
        functools.partial(win_kernel, ratio, middle),
        (facts, weight, queries, *own, rival_keys, rival_values, first_part),
        [VMEM] * 9,
        (second_shape, part_shape),
        (VMEM, VMEM),
        buffers(1),
        share * middle,
    )
    wide_shape = jax.ShapeDtypeStruct((groups, 2 * span, HD + LANES), dtype)
    second, part, *wide = kernel_call(
        functools.partial(lose_kernel, ratio, middle),
        (facts, weight, companion_keys, companion_values, rival_keys, rival_values, pieces[0], first_part, second, part),
        [VMEM] * 10,
        (second_shape, part_shape, wide_shape, wide_shape),
        (VMEM,) * 4,
        (),
        share * middle,
        {8: 0, 9: 1},
    )
    first, second, lost = kernel_call(
        functools.partial(last_kernel, ratio, middle),
        (facts, *wide, pieces[1], first, second),
        [VMEM] * 6,
        (first_shape, second_shape, second_shape),
        (ANY, ANY, VMEM),
        [pltpu.SemaphoreType.DMA((3 + LAST_HEADS,))],
        share // 16,
    )

    cores = lax.axis_size("head")
    devices = lax.axis_size("cand") * cores
    diagonal = [(i, i ^ (cores + 1)) for i in range(devices)]
    across = from_partner(part, "cand", 0)
    across_beside = lax.ppermute(part, ("cand", "head"), diagonal)
    beside = from_partner(part, "head", 0)
    score_shape = jax.ShapeDtypeStruct((1,), jnp.float32)
    second, first_score, final_round_score = kernel_call(
        final_kernel,
        (facts, part, beside, across, across_beside, lost, second),
        [VMEM] * 6 + [ANY],
        (second_shape, score_shape, score_shape),
        (ANY, ANY, ANY),
        [pltpu.SMEM((1,), jnp.float32)] * 2 + [pltpu.SemaphoreType.DMA((3,))],
        share // 16,
        {6: 0},
    )
    return first, second, first_score, final_round_score


def solution(mesh):
    in_specs = (
        P(("grp", "cand"), "head"),
        P(("grp", "cand"), "head"),
        P(("grp", "cand"), "head"),
        P("grp"),
        P("grp"),
        P("head"),
    )
    out_specs = (
        P(("grp", "cand"), "head"),
        P(("grp", "cand"), "head"),
        P(("grp", "cand")),
        P(("grp", "cand")),
    )
    return jax.shard_map(body, mesh=mesh, in_specs=in_specs, out_specs=out_specs, check_vma=False)
```

```python
import functools

import jax
import jax.numpy as jnp
from jax import lax
from jax.experimental import pallas as pl
from jax.experimental.pallas import tpu as pltpu
from jax.sharding import PartitionSpec as P

HD = 128
LANES = 128
LOG2E = 1.4426950408889634
FACTOR = HD ** (-0.5) * LOG2E
BARRED = -1e30
LAST_HEADS = 5
COST = 10
VMEM_LIMIT = 12 * 1024 * 1024
ANY = pl.BlockSpec(memory_space=pl.ANY)
HBM = pl.BlockSpec(memory_space=pltpu.HBM)
VMEM = pl.BlockSpec(memory_space=pltpu.VMEM)


def from_partner(value, axis, stride):
    return lax.ppermute(value, axis, [(i, i ^ 1 << stride) for i in range(lax.axis_size(axis))])


OWN_VALID, PARTNER_VALID, RIVAL_VALID, WON = range(4)


def gather_facts(lengths_ref, winners_ref):
    device = lax.axis_index("cand")
    pair = device >> 1
    rival_pair = pair ^ 1
    rival = 2 * rival_pair + winners_ref[rival_pair]
    won = jnp.where(winners_ref[pair] == (device & 1), 1, 0)
    row = lax.broadcasted_iota(jnp.int32, (8, LANES), 0)
    facts = jnp.zeros((8, LANES), jnp.int32)
    for index, number in enumerate((lengths_ref[device], lengths_ref[device ^ 1], lengths_ref[rival], won)):
        facts = jnp.where(row == index, number, facts)
    return facts.astype(jnp.float32)


def valid_of(facts_ref, index):
    return facts_ref[index : index + 1, :].astype(jnp.int32)


def has_won(facts_ref):
    return jnp.max(facts_ref[WON : WON + 1, :]) > 0.5


def load_span(k_buf, v_buf, k_ref, v_ref, group, valid, start):
    span = k_ref.shape[0]
    k_columns = slice(group * HD, (group + 1) * HD)
    v_columns = k_columns if v_ref.shape[1] == k_ref.shape[1] else slice(0, HD)
    rows = slice(start, start + span)
    row = lax.broadcasted_iota(jnp.int32, (span, LANES), 0)
    first_lane = lax.broadcasted_iota(jnp.int32, (span, LANES), 1) == 0
    k_buf[rows, :HD] = k_ref[:, k_columns]
    k_buf[rows, HD:] = jnp.where(first_lane & (row >= valid), BARRED, 0.0).astype(k_buf.dtype)
    v_buf[rows, :HD] = v_ref[:, v_columns]
    v_buf[rows, HD:] = jnp.ones((span, LANES), v_buf.dtype)


def score_rows(q, k_buf):
    lane = lax.broadcasted_iota(jnp.int32, (q.shape[0], LANES), 1)
    one_lane = jnp.where(lane == 0, 1.0, 0.0).astype(q.dtype)
    wide_q = jnp.concatenate([q, one_lane], axis=1)
    return lax.dot_general(wide_q, k_buf[...], (((1,), (1,)), ((), ())), preferred_element_type=jnp.float32)


def weigh(scores, peak, v_buf):
    wide_peak = jnp.concatenate([peak] * (scores.shape[1] // LANES), axis=1)
    exps = jnp.exp2(scores * FACTOR - wide_peak).astype(v_buf.dtype)
    both = jnp.dot(exps, v_buf[...], preferred_element_type=jnp.float32)
    return both[:, :HD], both[:, HD:]


def peak_of(scores):
    peak = jnp.max(scores, axis=1, keepdims=True) * FACTOR
    return jnp.broadcast_to(peak, (scores.shape[0], LANES))


def finish(above, below, valid_rows, first_row, dtype):
    row = lax.broadcasted_iota(jnp.int32, above.shape, 0) + first_row
    return jnp.where(row < valid_rows, above / below, 0.0).astype(dtype)


def in_turn(works):
    scores = works[0][0]()
    for index, (_, finish_work) in enumerate(works):
        later = works[index + 1][0]() if index + 1 < len(works) else None
        finish_work(scores)
        scores = later


def own_kernel(ratio, block, cuts, lengths_hbm, winners_hbm, q_hbm, k_hbm, v_hbm, o_ref, sum_ref, peak_ref, facts_ref, *rest):
    piece_refs, (q_ref, k_ref, v_ref, lengths_ref, winners_ref, k_buf, v_buf, sems) = rest[: len(cuts)], rest[len(cuts) :]
    groups = k_ref.shape[1] // HD
    lengths_copy = pltpu.make_async_copy(lengths_hbm, lengths_ref, sems.at[2 + groups])
    winners_copy = pltpu.make_async_copy(winners_hbm, winners_ref, sems.at[3 + groups])
    lengths_copy.start()
    winners_copy.start()
    copies = [pltpu.make_async_copy(k_hbm, k_ref, sems.at[0]), pltpu.make_async_copy(v_hbm, v_ref, sems.at[1])]
    for group in range(groups):
        columns = pl.ds(group * ratio * HD, ratio * HD)
        copies.append(pltpu.make_async_copy(q_hbm.at[:, columns], q_ref.at[:, columns], sems.at[2 + group]))
    for copy in copies:
        copy.start()
    lengths_copy.wait()
    winners_copy.wait()
    facts_ref[...] = gather_facts(lengths_ref, winners_ref)
    copies[0].wait()
    copies[1].wait()
    device = lax.axis_index("cand")
    half = q_ref.shape[0] // 2
    sent = pl.ds(pl.multiple_of((1 - (device & 1)) * half, half), half)
    for group in range(groups):
        load_span(k_buf.at[group], v_buf.at[group], k_ref, v_ref, group, valid_of(facts_ref, OWN_VALID), 0)

    def score(rows, columns, group):
        if rows.start == 0 and columns.start == group * ratio * HD:
            copies[2 + group].wait()
        return score_rows(q_ref[rows, columns], k_buf.at[group])

    def weigh_own(rows, columns, group, scores):
        peak = peak_of(scores)
        o_ref[rows, columns], sum_ref[rows, columns] = weigh(scores, peak, v_buf.at[group])
        peak_ref[rows, columns] = peak

    works = []
    for head in range(groups * ratio):
        for start in range(0, q_ref.shape[0], block):
            place = (slice(start, start + block), slice(head * HD, (head + 1) * HD), head // ratio)
            works.append((functools.partial(score, *place), functools.partial(weigh_own, *place)))
    in_turn(works)
    for piece_ref, (low, high) in zip(piece_refs, cuts):
        piece_ref[...] = q_ref[sent, low * HD : high * HD]


def choose_kernel(facts_ref, own_ref, companion_ref, out_ref):
    won = has_won(facts_ref)

    @pl.when(won)
    def _():
        out_ref[...] = own_ref[...]

    @pl.when(jnp.logical_not(won))
    def _():
        out_ref[...] = companion_ref[...]


def join_work(rows, first_row, columns, valid_rows, q_ref, own_refs, k_buf, v_buf, totals, keep_output):
    o_ref, sum_ref, peak_ref = own_refs

    def score():
        return score_rows(q_ref[rows, columns], k_buf)

    def join(scores):
        own_peak = peak_ref[rows, columns]
        peak = jnp.maximum(own_peak, peak_of(scores))
        above, below = weigh(scores, peak, v_buf)
        keep = jnp.exp2(own_peak - peak)
        above += o_ref[rows, columns] * keep
        below += sum_ref[rows, columns] * keep
        output = finish(above, below, valid_rows, first_row, q_ref.dtype)
        totals.append((columns, sum_rows(output)))
        keep_output(output)

    return score, join


def sum_rows(output):
    return jnp.sum(output.astype(jnp.float32).reshape(output.shape[0] // 8, 8, LANES), axis=0)


def weigh_totals(totals, weight_ref, facts_ref, index):
    valid = facts_ref[index : index + 1, :]
    score = jnp.zeros((8, LANES), jnp.float32)
    for columns, total in totals:
        score += total * weight_ref[:, columns]
    return jnp.full((8, LANES), jnp.sum(score), jnp.float32) / valid


def first_kernel(
    ratio, block, facts_ref, weight_ref, q_ref, o_ref, sum_ref, peak_ref, k_ref, v_ref,
    out_ref, part_ref, k_buf, v_buf, out_buf, sems,
):
    span, heads = q_ref.shape[0], q_ref.shape[1] // HD
    valid = valid_of(facts_ref, OWN_VALID)
    for group in range(heads // ratio):
        load_span(k_buf.at[group], v_buf.at[group], k_ref, v_ref, group, valid_of(facts_ref, PARTNER_VALID), 0)

    def out_copy(head):
        columns = pl.ds(head * HD, HD)
        return pltpu.make_async_copy(out_buf.at[:, columns], out_ref.at[:, columns], sems.at[head])

    def keep(rows, columns, output):
        out_buf[rows, columns] = output
        if rows.stop == span:
            out_copy(columns.start // HD).start()

    works, totals = [], []
    for head in range(heads):
        for start in range(0, span, block):
            rows, columns = slice(start, start + block), slice(head * HD, (head + 1) * HD)
            works.append(
                join_work(
                    rows, start, columns, valid, q_ref, (o_ref, sum_ref, peak_ref), k_buf.at[head // ratio],
                    v_buf.at[head // ratio], totals, functools.partial(keep, rows, columns),
                )
            )
    in_turn(works)
    part_ref[...] = weigh_totals(totals, weight_ref, facts_ref, OWN_VALID)
    for head in range(heads):
        out_copy(head).wait()


def lose_works(facts_ref, low, high, ratio, q_ref, k_buf, v_buf, totals, out_ref, then=None):
    half, span = q_ref.shape[0], k_buf.shape[1] // 2
    chunks, head = [], low
    while head < high:
        after = min(head + 2, high, (head // ratio + 1) * ratio)
        chunks.append(range(head, after))
        head = after

    def score(chunk):
        rows = jnp.concatenate([q_ref[:, (head - low) * HD : (head - low + 1) * HD] for head in chunk], axis=0)
        k_wide = k_buf.at[chunk[0] // ratio]
        return [score_rows(rows, k_wide.at[start : start + span]) for start in (0, span)]

    def attend(chunk, scores):
        v_wide = v_buf.at[chunk[0] // ratio]
        peak = jnp.maximum(*(jnp.max(each, axis=1, keepdims=True) for each in scores))
        both = 0.0
        for each, start in zip(scores, (0, span)):
            exps = jnp.exp2((each - peak) * FACTOR).astype(v_wide.dtype)
            both += jnp.dot(exps, v_wide[start : start + span], preferred_element_type=jnp.float32)
        first_row = (lax.axis_index("cand") & 1) * half
        for index, head in enumerate(chunk):
            columns = slice(head * HD, (head + 1) * HD)
            rows = both[index * half : (index + 1) * half]
            output = finish(rows[:, :HD], rows[:, HD:], valid_of(facts_ref, PARTNER_VALID), first_row, out_ref.dtype)
            totals.append((columns, sum_rows(output)))
            out_ref[:, columns] = output
            if then is not None:
                then(head)

    return [(functools.partial(score, chunk), functools.partial(attend, chunk)) for chunk in chunks]


def give_part(part_ref, part, first_ref):
    row = lax.broadcasted_iota(jnp.int32, part.shape, 0)
    part_ref[...] = jnp.where(row == 0, part, first_ref[...])


def win_kernel(
    ratio, low, facts_ref, weight_ref, q_ref, o_ref, sum_ref, peak_ref, k_ref, v_ref, first_ref, out_ref, part_ref, k_buf, v_buf
):
    half, heads = out_ref.shape[0], q_ref.shape[1] // HD

    @pl.when(has_won(facts_ref))
    def _():
        for group in range(heads // ratio):
            load_span(k_buf.at[group], v_buf.at[group], k_ref, v_ref, group, valid_of(facts_ref, RIVAL_VALID), 0)
        totals = []

        def keep(head, output):
            out_ref[:, head * HD : (head + 1) * HD] = output

        def work(head, start, keep_output):
            return join_work(
                pl.ds(start, half), start, slice(head * HD, (head + 1) * HD), valid_of(facts_ref, OWN_VALID), q_ref,
                (o_ref, sum_ref, peak_ref), k_buf.at[head // ratio], v_buf.at[head // ratio], totals, keep_output,
            )

        own_row = pl.multiple_of((lax.axis_index("cand") & 1) * half, half)
        other_row = pl.multiple_of(half - own_row, half)
        works = [work(head, own_row, functools.partial(keep, head)) for head in range(heads)]
        works += [work(head, other_row, lambda output: None) for head in range(low, heads)]
        in_turn(works)
        give_part(part_ref, weigh_totals(totals, weight_ref, facts_ref, OWN_VALID), first_ref)


def lose_kernel(
    ratio, high, facts_ref, weight_ref, ka_ref, va_ref, kb_ref, vb_ref, piece_ref, first_ref, second_ref, won_part_ref,
    out_ref, part_ref, second_out, k_wide, v_wide, sems,
):
    span = ka_ref.shape[0]

    def lost_copy(head):
        columns = pl.ds(head * HD, HD)
        return pltpu.make_async_copy(out_ref.at[:, columns], second_out.at[:, columns], sems.at[head])

    @pl.when(jnp.logical_not(has_won(facts_ref)))
    def _():
        for group in range(k_wide.shape[0]):
            own_k, own_v = k_wide.at[group], v_wide.at[group]
            load_span(own_k, own_v, ka_ref, va_ref, group, valid_of(facts_ref, PARTNER_VALID), 0)
            load_span(own_k, own_v, kb_ref, vb_ref, group, valid_of(facts_ref, RIVAL_VALID), span)
        totals = []
        works = lose_works(
            facts_ref, 0, high, ratio, piece_ref, k_wide, v_wide, totals, out_ref, lambda head: lost_copy(head).start()
        )
        in_turn(works)
        give_part(part_ref, weigh_totals(totals, weight_ref, facts_ref, PARTNER_VALID), first_ref)
        for head in range(high):
            lost_copy(head).wait()


def last_kernel(
    ratio, low, facts_ref, k_wide, v_wide, piece_ref, second_ref, before_ref, second_out, out_ref, sem
):
    won = has_won(facts_ref)

    @pl.when(won)
    def _():
        won_copy = pltpu.make_async_copy(second_ref, second_out, sem)
        won_copy.start()
        won_copy.wait()

    @pl.when(jnp.logical_not(won))
    def _():
        heads = out_ref.shape[1] // HD
        in_turn(lose_works(facts_ref, low, heads, ratio, piece_ref, k_wide, v_wide, [], out_ref))


def final_kernel(
    facts_ref, part_ref, beside_ref, across_ref, diagonal_ref, lost_ref, _, second_out, first_score, final_score,
    first_buf, final_buf, sems,
):
    won = has_won(facts_ref)
    width = LAST_HEADS * HD
    columns = pl.ds(second_out.shape[1] - width, width)
    tail_copy = pltpu.make_async_copy(lost_ref.at[:, columns], second_out.at[:, columns], sems.at[2])

    @pl.when(jnp.logical_not(won))
    def _():
        tail_copy.start()

    beside = part_ref[...] + beside_ref[...]
    total = beside + (across_ref[...] + diagonal_ref[...])
    score_copies = []
    scores = ((beside[1:2, :], first_buf, first_score), (total[0:1, :], final_buf, final_score))
    for index, (score, buf, out) in enumerate(scores):
        buf[0] = jnp.max(score)
        copy = pltpu.make_async_copy(buf, out, sems.at[index])
        copy.start()
        score_copies.append(copy)
    for copy in score_copies:
        copy.wait()

    @pl.when(jnp.logical_not(won))
    def _():
        tail_copy.wait()


def kernel_call(kernel, operands, in_specs, out_shape, out_specs, scratch=(), flops=0, aliases=None):
    return pl.pallas_call(
        kernel,
        out_shape=out_shape,
        in_specs=in_specs,
        out_specs=out_specs,
        scratch_shapes=scratch,
        input_output_aliases=aliases or {},
        compiler_params=pltpu.CompilerParams(vmem_limit_bytes=VMEM_LIMIT),
        cost_estimate=pl.CostEstimate(flops=COST * flops, bytes_accessed=COST * flops // 256, transcendentals=flops // 512),
    )(*operands)


def body(queries, keys, values, lengths, winners, score_weight):
    span, width = queries.shape
    half = span // 2
    heads = width // HD
    groups = keys.shape[1] // HD
    ratio = heads // groups
    block = min(span, 256)
    dtype = queries.dtype
    weight = score_weight.reshape(1, -1)
    share = 4 * span * span * HD
    part_shape = jax.ShapeDtypeStruct((8, LANES), jnp.float32)
    second_shape = jax.ShapeDtypeStruct((half, width), dtype)

    def buffers(spans):
        return [pltpu.VMEM((groups, spans * span, HD + LANES), dtype)] * 2

    companion_keys = from_partner(keys, "cand", 0)
    companion_values = from_partner(values, "cand", 0)

    middle = heads - LAST_HEADS
    cuts = [(0, middle), (middle, heads)]
    piece_shapes = tuple(jax.ShapeDtypeStruct((half, (high - low) * HD), dtype) for low, high in cuts)
    partial = jax.ShapeDtypeStruct((span, width), jnp.float32)
    *own, sent = kernel_call(
        functools.partial(own_kernel, ratio, block, cuts),
        [pltpu.with_memory_space_constraint(array, pltpu.HBM) for array in (lengths, winners, queries, keys, values)],
        [HBM] * 5,
        (partial,) * 3 + (part_shape,) + piece_shapes,
        (VMEM,) * (4 + len(cuts)),
        [pltpu.VMEM(array.shape, dtype) for array in (queries, keys, values)]
        + [pltpu.SMEM(array.shape, array.dtype) for array in (lengths, winners)]
        + buffers(1)
        + [pltpu.SemaphoreType.DMA((4 + groups,))],
        share * heads,
    )
    own, facts, sent = own[:3], own[3], own[4:] + [sent]

    pieces = [from_partner(piece, "cand", 0) for piece in sent]

    def choose(own, companion):
        shape = jax.ShapeDtypeStruct(own.shape, dtype)
        return kernel_call(choose_kernel, (facts, own, companion), [VMEM] * 3, shape, VMEM)

    chosen_keys = choose(keys, companion_keys)
    rival_keys = from_partner(chosen_keys, "cand", 1)
    companion_values, _ = lax.optimization_barrier((companion_values, chosen_keys))
    rival_values = from_partner(choose(values, companion_values), "cand", 1)

    first_shape = jax.ShapeDtypeStruct((span, width), dtype)
    first, first_part = kernel_call(
        functools.partial(first_kernel, ratio, block),
        (facts, weight, queries, *own, companion_keys, companion_values),
        [VMEM] * 8,
        (first_shape, part_shape),
        (ANY, VMEM),
        buffers(1) + [pltpu.VMEM((span, width), dtype), pltpu.SemaphoreType.DMA((heads,))],
        share * heads // 2,
    )
    second, part = kernel_call(
        functools.partial(win_kernel, ratio, middle),
        (facts, weight, queries, *own, rival_keys, rival_values, first_part),
        [VMEM] * 9,
        (second_shape, part_shape),
        (VMEM, VMEM),
        buffers(1),
        share * middle,
    )
    wide_shape = jax.ShapeDtypeStruct((groups, 2 * span, HD + LANES), dtype)
    second, part, before, *wide = kernel_call(
        functools.partial(lose_kernel, ratio, middle),
        (facts, weight, companion_keys, companion_values, rival_keys, rival_values, pieces[0], first_part, second, part),
        [VMEM] * 10,
        (second_shape, part_shape, second_shape, wide_shape, wide_shape),
        (VMEM, VMEM, ANY, VMEM, VMEM),
        [pltpu.SemaphoreType.DMA((middle,))],
        share * middle,
        {8: 0, 9: 1},
    )
    second, lost = kernel_call(
        functools.partial(last_kernel, ratio, middle),
        (facts, *wide, pieces[1], second, before),
        [VMEM] * 5 + [ANY],
        (second_shape, second_shape),
        (ANY, VMEM),
        [pltpu.SemaphoreType.DMA(())],
        share // 16,
        {5: 0},
    )

    cores = lax.axis_size("head")
    devices = lax.axis_size("cand") * cores
    diagonal = [(i, i ^ (cores + 1)) for i in range(devices)]
    across = from_partner(part, "cand", 0)
    across_beside = lax.ppermute(part, ("cand", "head"), diagonal)
    beside = from_partner(part, "head", 0)
    score_shape = jax.ShapeDtypeStruct((1,), jnp.float32)
    second, first_score, final_round_score = kernel_call(
        final_kernel,
        (facts, part, beside, across, across_beside, lost, second),
        [VMEM] * 6 + [ANY],
        (second_shape, score_shape, score_shape),
        (ANY, ANY, ANY),
        [pltpu.SMEM((1,), jnp.float32)] * 2 + [pltpu.SemaphoreType.DMA((3,))],
        share // 16,
        {6: 0},
    )
    return first, second, first_score, final_round_score


def solution(mesh):
    in_specs = (
        P(("grp", "cand"), "head"),
        P(("grp", "cand"), "head"),
        P(("grp", "cand"), "head"),
        P("grp"),
        P("grp"),
        P("head"),
    )
    out_specs = (
        P(("grp", "cand"), "head"),
        P(("grp", "cand"), "head"),
        P(("grp", "cand")),
        P(("grp", "cand")),
    )
    return jax.shard_map(body, mesh=mesh, in_specs=in_specs, out_specs=out_specs, check_vma=False)
```

```python
import functools

import jax
import jax.numpy as jnp
from jax import lax
from jax.experimental import pallas as pl
from jax.experimental.pallas import tpu as pltpu
from jax.sharding import PartitionSpec as P

HD = 128
LANES = 128
LOG2E = 1.4426950408889634
FACTOR = HD ** (-0.5) * LOG2E
BARRED = -1e30
LAST_HEADS = 5
COST = 10
VMEM_LIMIT = 12 * 1024 * 1024
ANY = pl.BlockSpec(memory_space=pl.ANY)
HBM = pl.BlockSpec(memory_space=pltpu.HBM)
VMEM = pl.BlockSpec(memory_space=pltpu.VMEM)


def from_partner(value, axis, stride):
    return lax.ppermute(value, axis, [(i, i ^ 1 << stride) for i in range(lax.axis_size(axis))])


OWN_VALID, PARTNER_VALID, RIVAL_VALID, WON = range(4)


def gather_facts(lengths_ref, winners_ref):
    device = lax.axis_index("cand")
    pair = device >> 1
    rival_pair = pair ^ 1
    rival = 2 * rival_pair + winners_ref[rival_pair]
    won = jnp.where(winners_ref[pair] == (device & 1), 1, 0)
    row = lax.broadcasted_iota(jnp.int32, (8, LANES), 0)
    facts = jnp.zeros((8, LANES), jnp.int32)
    for index, number in enumerate((lengths_ref[device], lengths_ref[device ^ 1], lengths_ref[rival], won)):
        facts = jnp.where(row == index, number, facts)
    return facts.astype(jnp.float32)


def valid_of(facts_ref, index):
    return facts_ref[index : index + 1, :].astype(jnp.int32)


def has_won(facts_ref):
    return jnp.max(facts_ref[WON : WON + 1, :]) > 0.5


def load_span(k_buf, v_buf, k_ref, v_ref, group, valid, start):
    span = k_ref.shape[0]
    k_columns = slice(group * HD, (group + 1) * HD)
    v_columns = k_columns if v_ref.shape[1] == k_ref.shape[1] else slice(0, HD)
    rows = slice(start, start + span)
    row = lax.broadcasted_iota(jnp.int32, (span, LANES), 0)
    first_lane = lax.broadcasted_iota(jnp.int32, (span, LANES), 1) == 0
    k_buf[rows, :HD] = k_ref[:, k_columns]
    k_buf[rows, HD:] = jnp.where(first_lane & (row >= valid), BARRED, 0.0).astype(k_buf.dtype)
    v_buf[rows, :HD] = v_ref[:, v_columns]
    v_buf[rows, HD:] = jnp.ones((span, LANES), v_buf.dtype)


def score_rows(q, k_buf):
    lane = lax.broadcasted_iota(jnp.int32, (q.shape[0], LANES), 1)
    one_lane = jnp.where(lane == 0, 1.0, 0.0).astype(q.dtype)
    wide_q = jnp.concatenate([q, one_lane], axis=1)
    return lax.dot_general(wide_q, k_buf[...], (((1,), (1,)), ((), ())), preferred_element_type=jnp.float32)


def weigh(scores, peak, v_buf):
    wide_peak = jnp.concatenate([peak] * (scores.shape[1] // LANES), axis=1)
    exps = jnp.exp2(scores * FACTOR - wide_peak).astype(v_buf.dtype)
    both = jnp.dot(exps, v_buf[...], preferred_element_type=jnp.float32)
    return both[:, :HD], both[:, HD:]


def peak_of(scores):
    peak = jnp.max(scores, axis=1, keepdims=True) * FACTOR
    return jnp.broadcast_to(peak, (scores.shape[0], LANES))


def finish(above, below, valid_rows, first_row, dtype):
    row = lax.broadcasted_iota(jnp.int32, above.shape, 0) + first_row
    return jnp.where(row < valid_rows, above / below, 0.0).astype(dtype)


def in_turn(works, scores=None):
    scores = works[0][0]() if scores is None else scores
    for index, (_, finish_work) in enumerate(works):
        later = works[index + 1][0]() if index + 1 < len(works) else None
        finish_work(scores)
        scores = later


def own_kernel(ratio, block, cuts, lengths_hbm, winners_hbm, q_hbm, k_hbm, v_hbm, o_ref, sum_ref, peak_ref, facts_ref, *rest):
    piece_refs, (q_ref, k_ref, v_ref, lengths_ref, winners_ref, k_buf, v_buf, sems) = rest[: len(cuts)], rest[len(cuts) :]
    groups = k_ref.shape[1] // HD
    lengths_copy = pltpu.make_async_copy(lengths_hbm, lengths_ref, sems.at[2 + groups])
    winners_copy = pltpu.make_async_copy(winners_hbm, winners_ref, sems.at[3 + groups])
    lengths_copy.start()
    winners_copy.start()
    copies = [pltpu.make_async_copy(k_hbm, k_ref, sems.at[0]), pltpu.make_async_copy(v_hbm, v_ref, sems.at[1])]
    for group in range(groups):
        columns = pl.ds(group * ratio * HD, ratio * HD)
        copies.append(pltpu.make_async_copy(q_hbm.at[:, columns], q_ref.at[:, columns], sems.at[2 + group]))
    for copy in copies:
        copy.start()
    lengths_copy.wait()
    winners_copy.wait()
    facts_ref[...] = gather_facts(lengths_ref, winners_ref)
    copies[0].wait()
    copies[1].wait()
    device = lax.axis_index("cand")
    half = q_ref.shape[0] // 2
    sent = pl.ds(pl.multiple_of((1 - (device & 1)) * half, half), half)
    for group in range(groups):
        load_span(k_buf.at[group], v_buf.at[group], k_ref, v_ref, group, valid_of(facts_ref, OWN_VALID), 0)

    def score(rows, columns, group):
        if rows.start == 0 and columns.start == group * ratio * HD:
            copies[2 + group].wait()
        return score_rows(q_ref[rows, columns], k_buf.at[group])

    def weigh_own(rows, columns, group, scores):
        peak = peak_of(scores)
        o_ref[rows, columns], sum_ref[rows, columns] = weigh(scores, peak, v_buf.at[group])
        peak_ref[rows, columns] = peak

    works = []
    for head in range(groups * ratio):
        for start in range(0, q_ref.shape[0], block):
            place = (slice(start, start + block), slice(head * HD, (head + 1) * HD), head // ratio)
            works.append((functools.partial(score, *place), functools.partial(weigh_own, *place)))
    in_turn(works)
    for piece_ref, (low, high) in zip(piece_refs, cuts):
        piece_ref[...] = q_ref[sent, low * HD : high * HD]


def choose_kernel(facts_ref, own_ref, companion_ref, out_ref):
    won = has_won(facts_ref)

    @pl.when(won)
    def _():
        out_ref[...] = own_ref[...]

    @pl.when(jnp.logical_not(won))
    def _():
        out_ref[...] = companion_ref[...]


def join_work(rows, first_row, columns, valid_rows, q_ref, own_refs, k_buf, v_buf, totals, keep_output):
    o_ref, sum_ref, peak_ref = own_refs

    def score():
        return score_rows(q_ref[rows, columns], k_buf)

    def join(scores):
        own_peak = peak_ref[rows, columns]
        peak = jnp.maximum(own_peak, peak_of(scores))
        above, below = weigh(scores, peak, v_buf)
        keep = jnp.exp2(own_peak - peak)
        above += o_ref[rows, columns] * keep
        below += sum_ref[rows, columns] * keep
        output = finish(above, below, valid_rows, first_row, q_ref.dtype)
        totals.append((columns, sum_rows(output)))
        keep_output(output)

    return score, join


def sum_rows(output):
    return jnp.sum(output.astype(jnp.float32).reshape(output.shape[0] // 8, 8, LANES), axis=0)


def weigh_totals(totals, weight_ref, facts_ref, index):
    valid = facts_ref[index : index + 1, :]
    score = jnp.zeros((8, LANES), jnp.float32)
    for columns, total in totals:
        score += total * weight_ref[:, columns]
    return jnp.full((8, LANES), jnp.sum(score), jnp.float32) / valid


def first_kernel(
    ratio, block, facts_ref, weight_ref, q_ref, o_ref, sum_ref, peak_ref, k_ref, v_ref,
    out_ref, part_ref, k_buf, v_buf, out_buf, sems,
):
    span, heads = q_ref.shape[0], q_ref.shape[1] // HD
    valid = valid_of(facts_ref, OWN_VALID)
    for group in range(heads // ratio):
        load_span(k_buf.at[group], v_buf.at[group], k_ref, v_ref, group, valid_of(facts_ref, PARTNER_VALID), 0)

    def out_copy(head):
        columns = pl.ds(head * HD, HD)
        return pltpu.make_async_copy(out_buf.at[:, columns], out_ref.at[:, columns], sems.at[head])

    def keep(rows, columns, output):
        out_buf[rows, columns] = output
        if rows.stop == span:
            out_copy(columns.start // HD).start()

    works, totals = [], []
    for head in range(heads):
        for start in range(0, span, block):
            rows, columns = slice(start, start + block), slice(head * HD, (head + 1) * HD)
            works.append(
                join_work(
                    rows, start, columns, valid, q_ref, (o_ref, sum_ref, peak_ref), k_buf.at[head // ratio],
                    v_buf.at[head // ratio], totals, functools.partial(keep, rows, columns),
                )
            )
    in_turn(works)
    part_ref[...] = weigh_totals(totals, weight_ref, facts_ref, OWN_VALID)
    for head in range(heads):
        out_copy(head).wait()


def lose_works(facts_ref, low, high, ratio, q_ref, k_buf, v_buf, totals, out_ref, then=None):
    half, span = q_ref.shape[0], k_buf.shape[1] // 2
    chunks, head = [], low
    while head < high:
        after = min(head + 2, high, (head // ratio + 1) * ratio)
        chunks.append(range(head, after))
        head = after

    def score(chunk):
        rows = jnp.concatenate([q_ref[:, (head - low) * HD : (head - low + 1) * HD] for head in chunk], axis=0)
        k_wide = k_buf.at[chunk[0] // ratio]
        return [score_rows(rows, k_wide.at[start : start + span]) for start in (0, span)]

    def attend(chunk, scores):
        v_wide = v_buf.at[chunk[0] // ratio]
        peak = jnp.maximum(*(jnp.max(each, axis=1, keepdims=True) for each in scores))
        both = 0.0
        for each, start in zip(scores, (0, span)):
            exps = jnp.exp2((each - peak) * FACTOR).astype(v_wide.dtype)
            both += jnp.dot(exps, v_wide[start : start + span], preferred_element_type=jnp.float32)
        first_row = (lax.axis_index("cand") & 1) * half
        for index, head in enumerate(chunk):
            columns = slice(head * HD, (head + 1) * HD)
            rows = both[index * half : (index + 1) * half]
            output = finish(rows[:, :HD], rows[:, HD:], valid_of(facts_ref, PARTNER_VALID), first_row, out_ref.dtype)
            totals.append((columns, sum_rows(output)))
            out_ref[:, columns] = output
            if then is not None:
                then(head)

    return [(functools.partial(score, chunk), functools.partial(attend, chunk)) for chunk in chunks]


def give_part(part_ref, part, first_ref):
    row = lax.broadcasted_iota(jnp.int32, part.shape, 0)
    part_ref[...] = jnp.where(row == 0, part, first_ref[...])


def win_kernel(
    ratio, low, facts_ref, weight_ref, q_ref, o_ref, sum_ref, peak_ref, k_ref, v_ref, first_ref, out_ref, part_ref, k_buf, v_buf
):
    half, heads = out_ref.shape[0], q_ref.shape[1] // HD

    @pl.when(has_won(facts_ref))
    def _():
        for group in range(heads // ratio):
            load_span(k_buf.at[group], v_buf.at[group], k_ref, v_ref, group, valid_of(facts_ref, RIVAL_VALID), 0)
        totals = []

        def keep(head, output):
            out_ref[:, head * HD : (head + 1) * HD] = output

        def work(head, start, keep_output):
            return join_work(
                pl.ds(start, half), start, slice(head * HD, (head + 1) * HD), valid_of(facts_ref, OWN_VALID), q_ref,
                (o_ref, sum_ref, peak_ref), k_buf.at[head // ratio], v_buf.at[head // ratio], totals, keep_output,
            )

        own_row = pl.multiple_of((lax.axis_index("cand") & 1) * half, half)
        other_row = pl.multiple_of(half - own_row, half)
        works = [work(head, own_row, functools.partial(keep, head)) for head in range(heads)]
        works += [work(head, other_row, lambda output: None) for head in range(low, heads)]
        in_turn(works)
        give_part(part_ref, weigh_totals(totals, weight_ref, facts_ref, OWN_VALID), first_ref)


def lose_kernel(
    ratio, high, facts_ref, weight_ref, ka_ref, va_ref, kb_ref, vb_ref, piece_ref, first_ref, second_ref, won_part_ref,
    out_ref, part_ref, second_out, k_wide, v_wide, sems,
):
    span = ka_ref.shape[0]

    def lost_copy(head):
        columns = pl.ds(head * HD, HD)
        return pltpu.make_async_copy(out_ref.at[:, columns], second_out.at[:, columns], sems.at[head])

    @pl.when(jnp.logical_not(has_won(facts_ref)))
    def _():
        for group in range(k_wide.shape[0]):
            own_k, own_v = k_wide.at[group], v_wide.at[group]
            load_span(own_k, own_v, ka_ref, va_ref, group, valid_of(facts_ref, PARTNER_VALID), 0)
            load_span(own_k, own_v, kb_ref, vb_ref, group, valid_of(facts_ref, RIVAL_VALID), span)
        totals = []
        works = lose_works(
            facts_ref, 0, high, ratio, piece_ref, k_wide, v_wide, totals, out_ref, lambda head: lost_copy(head).start()
        )
        in_turn(works)
        give_part(part_ref, weigh_totals(totals, weight_ref, facts_ref, PARTNER_VALID), first_ref)
        for head in range(high):
            lost_copy(head).wait()


def last_kernel(
    ratio, low, facts_ref, k_wide, v_wide, piece_ref, second_ref, before_ref, second_out, out_ref, sem
):
    works = lose_works(facts_ref, low, out_ref.shape[1] // HD, ratio, piece_ref, k_wide, v_wide, [], out_ref)
    scores = works[0][0]()
    won = has_won(facts_ref)

    @pl.when(won)
    def _():
        won_copy = pltpu.make_async_copy(second_ref, second_out, sem)
        won_copy.start()
        won_copy.wait()

    @pl.when(jnp.logical_not(won))
    def _():
        in_turn(works, scores)


def final_kernel(
    facts_ref, part_ref, beside_ref, across_ref, diagonal_ref, lost_ref, _, second_out, first_score, final_score,
    first_buf, final_buf, sems,
):
    won = has_won(facts_ref)
    width = LAST_HEADS * HD
    columns = pl.ds(second_out.shape[1] - width, width)
    tail_copy = pltpu.make_async_copy(lost_ref.at[:, columns], second_out.at[:, columns], sems.at[2])

    @pl.when(jnp.logical_not(won))
    def _():
        tail_copy.start()

    beside = part_ref[...] + beside_ref[...]
    total = beside + (across_ref[...] + diagonal_ref[...])
    score_copies = []
    scores = ((beside[1:2, :], first_buf, first_score), (total[0:1, :], final_buf, final_score))
    for index, (score, buf, out) in enumerate(scores):
        buf[0] = jnp.max(score)
        copy = pltpu.make_async_copy(buf, out, sems.at[index])
        copy.start()
        score_copies.append(copy)
    for copy in score_copies:
        copy.wait()

    @pl.when(jnp.logical_not(won))
    def _():
        tail_copy.wait()


def kernel_call(kernel, operands, in_specs, out_shape, out_specs, scratch=(), flops=0, aliases=None):
    return pl.pallas_call(
        kernel,
        out_shape=out_shape,
        in_specs=in_specs,
        out_specs=out_specs,
        scratch_shapes=scratch,
        input_output_aliases=aliases or {},
        compiler_params=pltpu.CompilerParams(vmem_limit_bytes=VMEM_LIMIT),
        cost_estimate=pl.CostEstimate(flops=COST * flops, bytes_accessed=COST * flops // 256, transcendentals=flops // 512),
    )(*operands)


def body(queries, keys, values, lengths, winners, score_weight):
    span, width = queries.shape
    half = span // 2
    heads = width // HD
    groups = keys.shape[1] // HD
    ratio = heads // groups
    block = min(span, 256)
    dtype = queries.dtype
    weight = score_weight.reshape(1, -1)
    share = 4 * span * span * HD
    part_shape = jax.ShapeDtypeStruct((8, LANES), jnp.float32)
    second_shape = jax.ShapeDtypeStruct((half, width), dtype)

    def buffers(spans):
        return [pltpu.VMEM((groups, spans * span, HD + LANES), dtype)] * 2

    companion_keys = from_partner(keys, "cand", 0)
    companion_values = from_partner(values, "cand", 0)

    middle = heads - LAST_HEADS
    cuts = [(0, middle), (middle, heads)]
    piece_shapes = tuple(jax.ShapeDtypeStruct((half, (high - low) * HD), dtype) for low, high in cuts)
    partial = jax.ShapeDtypeStruct((span, width), jnp.float32)
    *own, sent = kernel_call(
        functools.partial(own_kernel, ratio, block, cuts),
        [pltpu.with_memory_space_constraint(array, pltpu.HBM) for array in (lengths, winners, queries, keys, values)],
        [HBM] * 5,
        (partial,) * 3 + (part_shape,) + piece_shapes,
        (VMEM,) * (4 + len(cuts)),
        [pltpu.VMEM(array.shape, dtype) for array in (queries, keys, values)]
        + [pltpu.SMEM(array.shape, array.dtype) for array in (lengths, winners)]
        + buffers(1)
        + [pltpu.SemaphoreType.DMA((4 + groups,))],
        share * heads,
    )
    own, facts, sent = own[:3], own[3], own[4:] + [sent]

    pieces = [from_partner(piece, "cand", 0) for piece in sent]

    def choose(own, companion):
        shape = jax.ShapeDtypeStruct(own.shape, dtype)
        return kernel_call(choose_kernel, (facts, own, companion), [VMEM] * 3, shape, VMEM)

    chosen_keys = choose(keys, companion_keys)
    rival_keys = from_partner(chosen_keys, "cand", 1)
    companion_values, _ = lax.optimization_barrier((companion_values, chosen_keys))
    rival_values = from_partner(choose(values, companion_values), "cand", 1)

    first_shape = jax.ShapeDtypeStruct((span, width), dtype)
    first, first_part = kernel_call(
        functools.partial(first_kernel, ratio, block),
        (facts, weight, queries, *own, companion_keys, companion_values),
        [VMEM] * 8,
        (first_shape, part_shape),
        (ANY, VMEM),
        buffers(1) + [pltpu.VMEM((span, width), dtype), pltpu.SemaphoreType.DMA((heads,))],
        share * heads // 2,
    )
    second, part = kernel_call(
        functools.partial(win_kernel, ratio, middle),
        (facts, weight, queries, *own, rival_keys, rival_values, first_part),
        [VMEM] * 9,
        (second_shape, part_shape),
        (VMEM, VMEM),
        buffers(1),
        share * middle,
    )
    wide_shape = jax.ShapeDtypeStruct((groups, 2 * span, HD + LANES), dtype)
    second, part, before, *wide = kernel_call(
        functools.partial(lose_kernel, ratio, middle),
        (facts, weight, companion_keys, companion_values, rival_keys, rival_values, pieces[0], first_part, second, part),
        [VMEM] * 10,
        (second_shape, part_shape, second_shape, wide_shape, wide_shape),
        (VMEM, VMEM, ANY, VMEM, VMEM),
        [pltpu.SemaphoreType.DMA((middle,))],
        share * middle,
        {8: 0, 9: 1},
    )
    second, lost = kernel_call(
        functools.partial(last_kernel, ratio, middle),
        (facts, *wide, pieces[1], second, before),
        [VMEM] * 5 + [ANY],
        (second_shape, second_shape),
        (ANY, VMEM),
        [pltpu.SemaphoreType.DMA(())],
        share // 16,
        {5: 0},
    )

    cores = lax.axis_size("head")
    devices = lax.axis_size("cand") * cores
    diagonal = [(i, i ^ (cores + 1)) for i in range(devices)]
    across = from_partner(part, "cand", 0)
    across_beside = lax.ppermute(part, ("cand", "head"), diagonal)
    beside = from_partner(part, "head", 0)
    score_shape = jax.ShapeDtypeStruct((1,), jnp.float32)
    second, first_score, final_round_score = kernel_call(
        final_kernel,
        (facts, part, beside, across, across_beside, lost, second),
        [VMEM] * 6 + [ANY],
        (second_shape, score_shape, score_shape),
        (ANY, ANY, ANY),
        [pltpu.SMEM((1,), jnp.float32)] * 2 + [pltpu.SemaphoreType.DMA((3,))],
        share // 16,
        {6: 0},
    )
    return first, second, first_score, final_round_score


def solution(mesh):
    in_specs = (
        P(("grp", "cand"), "head"),
        P(("grp", "cand"), "head"),
        P(("grp", "cand"), "head"),
        P("grp"),
        P("grp"),
        P("head"),
    )
    out_specs = (
        P(("grp", "cand"), "head"),
        P(("grp", "cand"), "head"),
        P(("grp", "cand")),
        P(("grp", "cand")),
    )
    return jax.shard_map(body, mesh=mesh, in_specs=in_specs, out_specs=out_specs, check_vma=False)
```
